32 devices in a mesh: groups: 2 (over x), dom: 16 (over z, y, core).
Axes of the slice: x: 2, y: 2, z: 4, core: 2. Of those that a mesh axis runs over, the one named last changes fastest.
Arguments:
- cells: bfloat16 [32768, 256], P(('groups', 'dom')), parts along dimension 0, may hold values from -6 to 6
- counts: int32 [32], P(('groups', 'dom')), parts along dimension 0, may hold values from 256 to 1024, as said below
- w_x: bfloat16 [256, 256], replicated, may hold values from -0.375 to 0.375
- w_fx: bfloat16 [256, 256], replicated, may hold values from -0.375 to 0.375
- w_slice: bfloat16 [32, 64], replicated, may hold values from -3.59375 to 3.59375
- w_temp: bfloat16 [32], replicated, may hold values from -1.1953125 to 1.1953125
- w_qkv: bfloat16 [3, 32, 32], replicated, may hold values from -1 to 1
- w_out: bfloat16 [256, 256], replicated, may hold values from -0.375 to 0.375
- cotangent: bfloat16 [32768, 256], P(('groups', 'dom')), parts along dimension 0, may hold values from -6 to 6
Outputs:
- result: bfloat16 [32768, 256], P(('groups', 'dom')), parts along dimension 0
- grad_cells: bfloat16 [32768, 256], P(('groups', 'dom')), parts along dimension 0
- grad_w_x: float32 [512, 256], P('groups'), parts along dimension 0
- grad_w_fx: float32 [512, 256], P('groups'), parts along dimension 0
- grad_w_slice: float32 [64, 64], P('groups'), parts along dimension 0
- grad_w_temp: float32 [64], P('groups'), parts along dimension 0
- grad_w_qkv: float32 [6, 32, 32], P('groups'), parts along dimension 0
- grad_w_out: float32 [512, 256], P('groups'), parts along dimension 0
The draws below stay inside these ranges and needn't reach their ends.
There are 2 independent parts, one for each index of `groups`. The reference program is written for one: setup_inputs(seed, part) draws one part's arguments, and reference() takes and returns one part's arrays. A program takes and returns all parts, laid end to end along the dimension named above; an argument that names none is the same for every part. Nothing has to cross between parts.
Inputs may be any that keep to these rules, and one draw needn't show every extreme that they name: `counts`: entry p is the number of live cells of partition p; they are its first rows, the rest of its 1024 rows are padding; some partition is full.
All inputs are finite; a program needn't handle non-finite values.
Results may differ from the reference program's by a relative error of at most 0.012.
The reference program's roundings to bfloat16 on the way count: a program that leaves them out, or rounds other values in their place, can miss the bound.
Values may be sent and summed in bfloat16 or wider, within the bound.
A program may use at most 64 MiB of HBM per device.

```python
import math
import jax
import jax.numpy as jnp
from jax import lax

HEAD_DIM = 32
SLICES = 64
WIDTH = 256
ROW_CAPACITY = 1024
TOKENS = 16384
N_DOM = 16


def draw_counts(key, part):
    base = jax.random.randint(jax.random.fold_in(key, 11), (N_DOM,), ROW_CAPACITY // 4, ROW_CAPACITY + 1, dtype=jnp.int32)
    where = jax.random.randint(jax.random.fold_in(key, 23), (), 0, N_DOM, dtype=jnp.int32)
    return base.at[where].set(ROW_CAPACITY)


def block_levels(key, extent, split, smallest, high):
    level, own = 1.0, jax.random.fold_in(key, 6)
    for dim, parts in split:
        steps = jnp.exp(jax.random.uniform(jax.random.fold_in(own, dim), (parts,), jnp.float32, smallest / len(split), high / len(split)))
        level = level * jnp.repeat(steps, extent[dim] // parts).reshape([-1 if axis == dim else 1 for axis in range(len(extent))])
    return level


def scatter_about(stream_key, extent, width, bound, pieces=(), kind=jnp.bfloat16):
    array = jax.random.normal(stream_key, extent, jnp.float32) * width
    if len(pieces) > 0:
        array = block_levels(stream_key, extent, pieces, -0.22, 0.18) * array
    return jnp.clip(array, min=-bound, max=bound).astype(kind)


def setup_inputs(seed: int = 0, part: int = 0) -> dict:
    arg_keys = jax.random.split(jax.random.key(seed), 10)
    part_splits = jax.random.split(jax.random.fold_in(arg_keys[9], part), 10)
    cells = scatter_about(part_splits[0], (TOKENS, WIDTH), 1.0, 6.0, ((0, 16),))
    counts = draw_counts(jax.random.fold_in(jax.random.fold_in(arg_keys[9], part), 71), part)
    w_x = scatter_about(arg_keys[2], (WIDTH, WIDTH), WIDTH ** -0.5, 0.375)
    w_fx = scatter_about(arg_keys[3], (WIDTH, WIDTH), WIDTH ** -0.5, 0.375)
    w_slice = scatter_about(arg_keys[4], (HEAD_DIM, SLICES), 0.6, 3.59375)
    w_temp = scatter_about(arg_keys[5], (HEAD_DIM,), 0.3, 1.1953125)
    w_qkv = scatter_about(arg_keys[6], (3, HEAD_DIM, HEAD_DIM), HEAD_DIM ** -0.5, 1.0)
    w_out = scatter_about(arg_keys[7], (WIDTH, WIDTH), WIDTH ** -0.5, 0.375)
    cotangent = scatter_about(part_splits[8], (TOKENS, WIDTH), 1.0, 6.0, ((0, 16),))
    return dict(cells=cells, counts=counts, w_x=w_x, w_fx=w_fx, w_slice=w_slice, w_temp=w_temp, w_qkv=w_qkv, w_out=w_out, cotangent=cotangent)


def matrix_product(form, left, right):
    return jnp.einsum(form, left.astype(jnp.float32), right.astype(jnp.float32))

def slice_softmax(logits, temp_lin):
    temper = 0.5 + jax.nn.softplus(temp_lin)
    scaled = 10.0 * jnp.tanh(logits / 10.0) / temper
    powers = jnp.exp(scaled)
    return powers / lax.optimization_barrier(jnp.sum(powers, axis=-1, keepdims=True))

def make_tokens(numerator_sums, denominators):
    return numerator_sums / (denominators[:, None] + 1e-05)

def project_tokens(tokens, qkv_weight):
    return jnp.einsum('rd,kde->kre', tokens, qkv_weight, precision=lax.Precision.HIGHEST)

def attend(query_rows, key_matrix, value_matrix):
    score_matrix = jnp.einsum('zir,zjr->zij', query_rows, key_matrix, precision=lax.Precision.HIGHEST)
    score_matrix = score_matrix / math.sqrt(query_rows.shape[-1])
    powers = jnp.exp(10.0 * jnp.tanh(score_matrix / 10.0))
    attention_matrix = powers / lax.optimization_barrier(jnp.sum(powers, axis=-1, keepdims=True))
    return jnp.einsum('xwu,xut->xwt', attention_matrix, value_matrix, precision=lax.Precision.HIGHEST)

def mix_tokens(numerator_sums, denominators, qkv_weight):
    head_width = numerator_sums.shape[-1]
    maps = project_tokens(make_tokens(numerator_sums, denominators), qkv_weight)
    maps = maps.reshape(3, -1, SLICES, head_width)
    return attend(maps[0], maps[1], maps[2])

def cell_forward(cells, live_rows, w_x, w_fx, w_slice, w_temp):
    count_of_rows = cells.shape[0]
    head_width = w_slice.shape[0]
    count_of_heads = w_x.shape[1] // head_width
    projected = jnp.dot(cells, w_x, preferred_element_type=jnp.float32).astype(jnp.bfloat16)
    feature_rows = jnp.dot(cells, w_fx, preferred_element_type=jnp.float32).astype(jnp.bfloat16)
    per_head = projected.reshape(count_of_rows * count_of_heads, head_width)
    logits = jnp.dot(per_head, w_slice, preferred_element_type=jnp.float32)
    temp_lin = jnp.dot(per_head, w_temp.reshape(head_width, 1), preferred_element_type=jnp.float32)
    live_heads = jnp.repeat(live_rows, count_of_heads, axis=0)
    weight_matrix = (slice_softmax(logits, temp_lin) * live_heads).astype(jnp.bfloat16)
    weight_matrix = weight_matrix.reshape(count_of_rows, count_of_heads, -1)
    return (per_head, logits, temp_lin, live_heads, weight_matrix, feature_rows.reshape(count_of_rows, count_of_heads, head_width))

def cell_backward(cells, per_head, logits, temp_lin, live_heads, weight_matrix, feature_rows, hidden_gradient3, mixed_lowp, numerator_gradient_lowp, denominator_gradient, w_x, w_fx, w_slice, w_temp):
    count_of_rows, count_of_heads, slice_count = weight_matrix.shape
    head_width = w_slice.shape[0]
    weight_gradient = matrix_product('fvo,vxo->fvx', hidden_gradient3, mixed_lowp)
    weight_gradient = weight_gradient + matrix_product('fvo,vxo->fvx', feature_rows, numerator_gradient_lowp) + denominator_gradient[None]
    feature_gradient = matrix_product('rpc,pce->rpe', weight_matrix, numerator_gradient_lowp).astype(jnp.bfloat16).reshape(count_of_rows, -1)
    _, soft_back = jax.vjp(slice_softmax, logits, temp_lin)
    d_logits, d_temp = soft_back(weight_gradient.reshape(count_of_rows * count_of_heads, slice_count) * live_heads)
    d_logits = d_logits.astype(jnp.bfloat16)
    d_temp = d_temp.astype(jnp.bfloat16)
    d_head = jnp.dot(d_logits, w_slice.T, preferred_element_type=jnp.float32)
    d_head = d_head + jnp.dot(d_temp, w_temp.reshape(1, head_width), preferred_element_type=jnp.float32)
    d_proj = d_head.reshape(count_of_rows, -1).astype(jnp.bfloat16)
    grad_cells = jnp.dot(d_proj, w_x.T, preferred_element_type=jnp.float32)
    grad_cells = (grad_cells + jnp.dot(feature_gradient, w_fx.T, preferred_element_type=jnp.float32)).astype(jnp.bfloat16)
    grad_wx = jnp.dot(cells.T, d_proj, preferred_element_type=jnp.float32)
    grad_wfx = jnp.dot(cells.T, feature_gradient, preferred_element_type=jnp.float32)
    grad_slice = jnp.dot(per_head.T, d_logits, preferred_element_type=jnp.float32)
    grad_temp = jnp.dot(per_head.T, d_temp, preferred_element_type=jnp.float32).reshape(head_width)
    return (grad_cells, grad_wx, grad_wfx, grad_slice, grad_temp)

def reference(cells, counts, w_x, w_fx, w_slice, w_temp, w_qkv, w_out, cotangent):
    model_width = w_x.shape[0]
    head_width = w_slice.shape[0]
    count_of_heads = model_width // head_width
    blocks = cells.reshape(N_DOM, ROW_CAPACITY, model_width)
    cot_blocks = cotangent.reshape(N_DOM, ROW_CAPACITY, model_width)
    positions = jnp.arange(ROW_CAPACITY, dtype=jnp.int32)

    def live_of(count):
        return (positions < count).astype(jnp.float32)[:, None]

    def sums_of(item):
        block, count = item
        outs_fwd = cell_forward(block, live_of(count), w_x, w_fx, w_slice, w_temp)
        weight_matrix, feature_rows = (outs_fwd[4], outs_fwd[5])
        return (matrix_product('skb,sko->kbo', weight_matrix, feature_rows), lax.optimization_barrier(jnp.sum(weight_matrix.astype(jnp.float32), axis=0)))
    numer_all, denom_all = lax.map(sums_of, (blocks, counts.astype(jnp.int32)))
    numerator_sums = lax.optimization_barrier(jnp.sum(numer_all, axis=0))
    denominators = lax.optimization_barrier(jnp.sum(denom_all, axis=0))
    qkv_weight = w_qkv.astype(jnp.float32)
    mixed, mix_back = jax.vjp(mix_tokens, numerator_sums.reshape(-1, head_width), denominators.reshape(-1), qkv_weight)
    mixed_lowp = mixed.astype(jnp.bfloat16)

    def forward_of(item):
        block, count, cot_block = item
        outs_fwd = cell_forward(block, live_of(count), w_x, w_fx, w_slice, w_temp)
        weight_matrix = outs_fwd[4]
        hidden_rows = matrix_product('rpc,pce->rpe', weight_matrix, mixed_lowp).astype(jnp.bfloat16).reshape(ROW_CAPACITY, model_width)
        result = jnp.dot(hidden_rows, w_out, preferred_element_type=jnp.float32).astype(jnp.bfloat16)
        hidden_gradient = jnp.dot(cot_block, w_out.T, preferred_element_type=jnp.float32).astype(jnp.bfloat16)
        out_grad = jnp.dot(hidden_rows.T, cot_block, preferred_element_type=jnp.float32)
        mixed_gradient = matrix_product('skb,sko->kbo', weight_matrix, hidden_gradient.reshape(ROW_CAPACITY, count_of_heads, head_width))
        return (result, out_grad, mixed_gradient)
    results, out_grads, d_mixed_all = lax.map(forward_of, (blocks, counts.astype(jnp.int32), cot_blocks))
    d_numer, denominator_gradient, d_qkv = mix_back(lax.optimization_barrier(jnp.sum(d_mixed_all, axis=0)))
    numerator_gradient_lowp = d_numer.reshape(count_of_heads, -1, head_width).astype(jnp.bfloat16)
    denominator_gradient = denominator_gradient.reshape(count_of_heads, -1)

    def backward_of(item):
        block, count, cot_block = item
        per_head, logits, temp_lin, live_heads, weight_matrix, feature_rows = cell_forward(block, live_of(count), w_x, w_fx, w_slice, w_temp)
        hidden_gradient = jnp.dot(cot_block, w_out.T, preferred_element_type=jnp.float32).astype(jnp.bfloat16)
        return cell_backward(block, per_head, logits, temp_lin, live_heads, weight_matrix, feature_rows, hidden_gradient.reshape(ROW_CAPACITY, count_of_heads, head_width), mixed_lowp, numerator_gradient_lowp, denominator_gradient, w_x, w_fx, w_slice, w_temp)
    grad_cells, grad_wx, grad_wfx, grad_slice, grad_temp = lax.map(backward_of, (blocks, counts.astype(jnp.int32), cot_blocks))
    scale = 1.0 / math.sqrt(TOKENS)
    return (results.reshape(TOKENS, model_width), grad_cells.reshape(TOKENS, model_width), lax.optimization_barrier(jnp.sum(grad_wx, axis=0)) * scale, lax.optimization_barrier(jnp.sum(grad_wfx, axis=0)) * scale, lax.optimization_barrier(jnp.sum(grad_slice, axis=0)) * scale, lax.optimization_barrier(jnp.sum(grad_temp, axis=0)) * scale, d_qkv * scale, lax.optimization_barrier(jnp.sum(out_grads, axis=0)) * scale)
```

```python
import functools
import math

import jax
import jax.numpy as jnp
from jax import lax
from jax.experimental import pallas as pl
from jax.experimental.pallas import tpu as pltpu
from jax.sharding import PartitionSpec as P

HEAD = 32
SLICES = 64
HEADS = 8
WIDTH = HEAD * HEADS
SPREAD = SLICES * HEADS
HALF = WIDTH // 2
CHUNK = 256
F32 = jnp.float32
BF16 = jnp.bfloat16
MESH = pl.DeviceIdType.MESH


def mm(left, right):
    return jnp.dot(left, right, preferred_element_type=F32)


def mm_nt(left, right):
    return lax.dot_general(left, right, (((1,), (1,)), ((), ())), preferred_element_type=F32)


def mm_tn(left, right):
    return lax.dot_general(left, right, (((0,), (0,)), ((), ())), preferred_element_type=F32)


def split(value):
    high = value.astype(BF16)
    return high, (value - high.astype(F32)).astype(BF16)


def pick2(value, ones):
    high, low = split(value)
    return mm(high, ones) + mm(low, ones)


def pick3(value, ones, product=mm):
    high = value.astype(BF16)
    rest = value - high.astype(F32)
    middle, low = split(rest)
    return product(high, ones) + product(middle, ones) + product(low, ones)


def wide(left, right, product):
    left_high, left_low = split(left)
    right_high, right_low = split(right)
    return (
        product(left_high, right_high)
        + product(left_high, right_low)
        + product(left_low, right_high)
    )


def block_mask(shape, row_width, column_width):
    rows = lax.broadcasted_iota(jnp.int32, shape, 0)
    columns = lax.broadcasted_iota(jnp.int32, shape, 1)
    return (rows // row_width) == (columns // column_width)


def stages_of(devices, rows, tile):
    sizes, rest = [2], devices // 2
    while rest > 1:
        size = min(8, rest)
        sizes.append(size)
        rest //= size
    stages, stride = [], 1
    for size in sizes:
        scattered = rows % (size * tile) == 0
        stages.append((size, stride, rows, scattered))
        rows = rows // size if scattered else rows
        stride *= size
    return stages


def peers_of(stage):
    size, stride, _, _ = stage
    me = lax.axis_index("dom")
    place = lax.rem(lax.div(me, stride), size)
    others = []
    for step in range(1, size):
        there = lax.rem(place + step, size)
        others.append((there, me + (there - place) * stride))
    return place, others


class Reduction:
    @staticmethod
    def scratch(stages, columns, dtype):
        shapes = []
        for size, _, rows, scattered in stages:
            part = rows // size if scattered else rows
            shapes += [
                pltpu.VMEM((rows, columns), dtype),
                pltpu.VMEM((size, part, columns), dtype),
                pltpu.VMEM((rows, columns), dtype),
                pltpu.SemaphoreType.DMA((4, size)),
            ]
        return shapes

    def __init__(self, stages, refs):
        self.stages = stages
        self.levels = [refs[4 * i : 4 * i + 4] for i in range(len(stages))]

    def source(self):
        return self.levels[0][0]

    def total(self):
        return self.levels[0][2]

    def send(self, index):
        stage = self.stages[index]
        size, _, rows, scattered = stage
        source, received, _, sems = self.levels[index]
        place, others = peers_of(stage)
        part = rows // size if scattered else rows
        self.flying = []
        for step, (there, device) in enumerate(others):
            cut = source
            if scattered:
                cut = source.at[pl.ds(pl.multiple_of(there * part, part), part), :]
            copy = pltpu.make_async_remote_copy(
                src_ref=cut,
                dst_ref=received.at[place],
                send_sem=sems.at[0, step],
                recv_sem=sems.at[1, step],
                device_id={"dom": device},
                device_id_type=MESH,
            )
            copy.start()
            self.flying.append(copy)
        if scattered:
            received[place] = source[pl.ds(pl.multiple_of(place * part, part), part), :]
        else:
            received[place] = source[...]

    def fold(self, index):
        size, _, rows, scattered = self.stages[index]
        source, received, gathered, _ = self.levels[index]
        for copy in self.flying:
            copy.wait()
        total = received[0].astype(F32)
        for slot in range(1, size):
            total = total + received[slot].astype(F32)
        total = total.astype(source.dtype)
        if index + 1 < len(self.stages):
            self.levels[index + 1][0][...] = total
        else:
            self.place(index, total)

    def place(self, index, value):
        size, _, rows, scattered = self.stages[index]
        gathered = self.levels[index][2]
        if scattered:
            part = rows // size
            place, _ = peers_of(self.stages[index])
            gathered[pl.ds(pl.multiple_of(place * part, part), part), :] = value
        else:
            gathered[...] = value

    def gather(self, index):
        stage = self.stages[index]
        size, _, rows, scattered = stage
        gathered, sems = self.levels[index][2:]
        self.flying = []
        if not scattered:
            return
        part = rows // size
        place, others = peers_of(stage)
        mine = gathered.at[pl.ds(pl.multiple_of(place * part, part), part), :]
        for step, (_, device) in enumerate(others):
            copy = pltpu.make_async_remote_copy(
                src_ref=mine,
                dst_ref=mine,
                send_sem=sems.at[2, step],
                recv_sem=sems.at[3, step],
                device_id={"dom": device},
                device_id_type=MESH,
            )
            copy.start()
            self.flying.append(copy)

    def settle(self, index):
        for copy in self.flying:
            copy.wait()
        if index > 0:
            self.place(index - 1, self.levels[index][2][...])

    def last(self):
        return len(self.stages) - 1


def layer_kernel(
    token_stages,
    grad_stages,
    scale,
    counts_ref,
    cells_ref,
    cot_ref,
    wx_ref,
    wfx_ref,
    wslice_ref,
    wtemp_ref,
    wqkv_ref,
    wout_ref,
    result_ref,
    gcells_ref,
    gwx_ref,
    gwfx_ref,
    gslice_ref,
    gtemp_ref,
    gqkv_ref,
    gout_ref,
    proj_ref,
    feat_ref,
    dhid_ref,
    weight_ref,
    prob_ref,
    tanh_ref,
    scaled_ref,
    inverse_ref,
    sigmoid_ref,
    slice_bd,
    temp_bd,
    temp_row,
    acc_tokens,
    acc_out,
    acc_cells,
    acc_slice,
    acc_temp,
    mixed_bd,
    dnumer_bd,
    *sum_refs,
):
    rows = cells_ref.shape[0]
    chunks = rows // CHUNK
    levels = 4 * len(token_stages)
    levels_g = 4 * len(grad_stages)
    token_sum = Reduction(token_stages, sum_refs[:levels])
    early_sum = Reduction(grad_stages, sum_refs[levels : levels + levels_g])
    late_sum = Reduction(grad_stages, sum_refs[levels + levels_g :])

    barrier = pltpu.get_barrier_semaphore()
    greeted = 0
    for stage in token_stages:
        for _, device in peers_of(stage)[1]:
            pl.semaphore_signal(barrier, inc=1, device_id={"dom": device}, device_id_type=MESH)
            greeted += 1

    count = counts_ref[0]
    repeat32 = (
        (lax.broadcasted_iota(jnp.int32, (HEAD, WIDTH), 1) % HEAD)
        == lax.broadcasted_iota(jnp.int32, (HEAD, WIDTH), 0)
    ).astype(BF16)
    repeat64 = (
        (lax.broadcasted_iota(jnp.int32, (SLICES, SPREAD), 1) % SLICES)
        == lax.broadcasted_iota(jnp.int32, (SLICES, SPREAD), 0)
    ).astype(BF16)
    diag_slice = block_mask((WIDTH, SPREAD), HEAD, SLICES)
    tall = mm_tn(repeat32, wslice_ref[...]).astype(BF16)
    slice_bd[...] = jnp.where(diag_slice, mm(tall, repeat64), 0.0).astype(BF16)
    temp_rows = jnp.broadcast_to(wtemp_ref[...], (128, HEAD))
    temp_bd[...] = jnp.where(
        block_mask((WIDTH, 128), HEAD, 1), mm_nt(repeat32.T, temp_rows), 0.0
    ).astype(BF16)
    temp_row[...] = jnp.where(
        block_mask((128, WIDTH), 1, HEAD), mm(temp_rows, repeat32), 0.0
    ).astype(BF16)
    gather_heads = block_mask((SPREAD, 128), SLICES, 1).astype(BF16)
    spread_heads = block_mask((128, SPREAD), 1, SLICES).astype(BF16)
    half_diag = block_mask((256, HALF), SLICES, HEAD)

    acc_tokens[...] = jnp.zeros_like(acc_tokens)
    acc_out[...] = jnp.zeros_like(acc_out)
    acc_cells[...] = jnp.zeros_like(acc_cells)
    acc_slice[...] = jnp.zeros_like(acc_slice)
    acc_temp[...] = jnp.zeros_like(acc_temp)

    def cut(index):
        return pl.ds(pl.multiple_of(index * CHUNK, CHUNK), CHUNK)

    def live_of(index):
        place = lax.broadcasted_iota(jnp.int32, (CHUNK, 1), 0) + index * CHUNK
        return (place < count).astype(F32)

    def forward(index, carry):
        part = cut(index)
        cells = cells_ref[part, :]
        projected = mm(cells, wx_ref[...]).astype(BF16)
        features = mm(cells, wfx_ref[...]).astype(BF16)
        d_hidden = mm_nt(cot_ref[part, :], wout_ref[...]).astype(BF16)
        logits = mm(projected, slice_bd[...])
        temp_lin = mm(projected, temp_bd[...])
        away = jnp.exp(-jnp.abs(temp_lin))
        temper = 0.5 + (jnp.maximum(temp_lin, 0.0) + jnp.log(1.0 + away))
        inverse = 1.0 / temper
        sigmoid = jnp.where(temp_lin >= 0.0, 1.0, away) / (1.0 + away)
        bent = jnp.tanh(logits / 10.0)
        scaled = (10.0 * bent) * pick2(inverse, spread_heads)
        powers = jnp.exp(scaled)
        sums = pick2(powers, gather_heads)
        used = lax.broadcasted_iota(jnp.int32, (CHUNK, 128), 1) < HEADS
        over = live_of(index) / jnp.where(used, sums, 1.0)
        probs = powers * pick2(over, spread_heads)
        weights = probs.astype(BF16)
        proj_ref[part, :] = projected
        feat_ref[part, :] = features
        dhid_ref[part, :] = d_hidden
        weight_ref[part, :] = weights
        prob_ref[part, :] = probs
        tanh_ref[part, :] = bent
        scaled_ref[part, :] = scaled
        inverse_ref[part, :] = inverse
        sigmoid_ref[part, :] = sigmoid
        ones = jnp.ones((CHUNK, 128), BF16)
        for half in range(2):
            lanes = slice(half * HALF, (half + 1) * HALF)
            right = jnp.concatenate([features[:, lanes], d_hidden[:, lanes], ones], axis=1)
            acc_tokens[half] += mm_tn(weights[:, half * 256 : (half + 1) * 256], right)
        return carry

    lax.fori_loop(0, chunks, forward, 0)

    payload = token_sum.source()
    lane = lax.broadcasted_iota(jnp.int32, (SLICES, 128), 1)
    totals = jnp.zeros((SLICES, 128), F32)
    for half in range(2):
        lanes = slice(half * HALF, (half + 1) * HALF)
        numer = jnp.where(half_diag, acc_tokens[half, :, 0:HALF], 0.0)
        dmix = jnp.where(half_diag, acc_tokens[half, :, HALF : 2 * HALF], 0.0)
        payload[0:SLICES, lanes] = sum(numer[i * 64 : i * 64 + 64] for i in range(4))
        payload[SLICES : 2 * SLICES, lanes] = sum(dmix[i * 64 : i * 64 + 64] for i in range(4))
        for i in range(4):
            block = acc_tokens[half, i * 64 : i * 64 + 64, 2 * HALF : 2 * HALF + 128]
            totals = totals + jnp.where(lane == half * 4 + i, block, 0.0)
    payload[0:SLICES, WIDTH : WIDTH + 128] = totals
    payload[SLICES : 2 * SLICES, WIDTH : WIDTH + 128] = jnp.zeros((SLICES, 128), F32)

    pl.semaphore_wait(barrier, greeted)
    for index in range(len(token_stages)):
        token_sum.send(index)
        token_sum.fold(index)
    for index in reversed(range(len(token_stages))):
        token_sum.gather(index)
        token_sum.settle(index)

    total = token_sum.total()
    numerators = total[0:SLICES, 0:WIDTH]
    d_mixed = total[SLICES : 2 * SLICES, 0:WIDTH]
    spread32 = block_mask((128, WIDTH), 1, HEAD).astype(BF16)
    denominators = pick3(total[0:SLICES, WIDTH : WIDTH + 128], spread32) + 1e-05
    tokens = numerators / denominators
    diag_square = block_mask((WIDTH, WIDTH), HEAD, HEAD)
    diag_tall = block_mask((SPREAD, WIDTH), SLICES, HEAD)
    maps = []
    for k in range(3):
        stacked = mm_tn(repeat32, wqkv_ref[k]).astype(BF16)
        maps.append(jnp.where(diag_square, mm(stacked, repeat32), 0.0).astype(BF16))


    queries, key_rows, value_rows = [
        pick3(tokens, weight) for weight in maps
    ]

    def expand(value):
        return jnp.where(diag_tall, jnp.concatenate([value] * HEADS, axis=0), 0.0)

    def contract(value):
        value = jnp.where(diag_tall, value, 0.0)
        return sum(value[i * SLICES : (i + 1) * SLICES] for i in range(HEADS))

    keys_bd = expand(key_rows)
    values_bd = expand(value_rows)
    root = 1.0 / math.sqrt(HEAD)
    bent = jnp.tanh(wide(queries, keys_bd, mm_nt) * root / 10.0)
    powers = jnp.exp(10.0 * bent)
    sums = pick3(powers, gather_heads)
    used = lax.broadcasted_iota(jnp.int32, (SLICES, 128), 1) < HEADS
    attention = powers * pick3(1.0 / jnp.where(used, sums, 1.0), spread_heads)
    mixed_low = wide(attention, values_bd, mm).astype(BF16)
    mixed_bd[...] = expand(mixed_low.astype(F32)).astype(BF16)

    d_attention = wide(d_mixed, values_bd, mm_nt)
    d_values = contract(wide(attention, d_mixed, mm_tn))
    shared = attention * d_attention
    shared = shared - attention * pick3(pick3(shared, gather_heads), spread_heads)
    d_scores = shared * (1.0 - bent * bent) * root
    d_queries = wide(d_scores, keys_bd, mm)
    d_keys = contract(wide(d_scores, queries, mm_tn))
    d_maps = (d_queries, d_keys, d_values)
    d_tokens = sum(pick3(d, weight, mm_nt) for d, weight in zip(d_maps, maps))
    d_numer = d_tokens / denominators
    dnumer_bd[...] = expand(d_numer).astype(BF16)
    d_denom = pick3(
        -expand(d_numer * tokens), jnp.ones((128, WIDTH), BF16),
        lambda value, ones: mm_nt(ones, value),
    )[0:1, :]
    for k in range(3):
        square = jnp.where(diag_square, wide(tokens, d_maps[k], mm_tn), 0.0)
        strip = sum(square[i * HEAD : (i + 1) * HEAD] for i in range(HEADS))
        gqkv_ref[k] = pick3(strip, repeat32, mm_nt) * scale

    def early(index, carry):
        part = cut(index)
        weights = weight_ref[part, :]
        cot = cot_ref[part, :]
        hidden = mm(weights, mixed_bd[...]).astype(BF16)
        d_features = mm(weights, dnumer_bd[...]).astype(BF16)
        result_ref[part, :] = mm(hidden, wout_ref[...]).astype(BF16)
        dfeat = mm_nt(d_features, wfx_ref[...])
        acc_out[:, 0:WIDTH] += mm_tn(hidden, cot)
        acc_out[:, WIDTH : 2 * WIDTH] += mm_tn(cells_ref[part, :], d_features)
        scaled = scaled_ref[part, :]
        probs = prob_ref[part, :]
        bent = tanh_ref[part, :]
        inverse = inverse_ref[part, :]
        d_weights = (
            mm_nt(dhid_ref[part, :], mixed_bd[...])
            + mm_nt(feat_ref[part, :], dnumer_bd[...])
            + d_denom
        )
        shared = probs * d_weights
        shared = shared - probs * pick2(pick2(shared, gather_heads), spread_heads)
        d_logits = (
            shared * (1.0 - bent * bent) * pick2(inverse, spread_heads)
        ).astype(BF16)
        d_temper = -pick2(shared * scaled, gather_heads) * inverse
        d_temp = (d_temper * sigmoid_ref[part, :]).astype(BF16)
        d_proj = (mm_nt(d_logits, slice_bd[...]) + mm(d_temp, temp_row[...])).astype(BF16)
        gcells_ref[part, :] = (mm_nt(d_proj, wx_ref[...]) + dfeat).astype(BF16)
        acc_cells[...] += mm_tn(cells_ref[part, :], d_proj)
        projected = proj_ref[part, :]
        acc_temp[...] += mm_tn(projected, d_temp)
        for half in range(2):
            acc_slice[half] += mm_tn(
                projected[:, half * HALF : (half + 1) * HALF],
                d_logits[:, half * 256 : (half + 1) * 256],
            )
        return carry

    lax.fori_loop(0, chunks, early, 0)

    early_sum.source()[...] = acc_out[...].astype(BF16)
    early_sum.send(0)
    late = late_sum.source()
    late[:, 0:WIDTH] = acc_cells[...].astype(BF16)
    own = jnp.where(block_mask((WIDTH, 128), HEAD, 1), acc_temp[...], 0.0)
    own = jnp.sum(own, axis=1, keepdims=True)
    for half in range(2):
        block = jnp.where(block_mask((HALF, 256), HEAD, SLICES), acc_slice[half], 0.0)
        block = block[:, 0:128] + block[:, 128:256]
        block = block + pltpu.roll(block, 64, 1)
        lanes = lax.broadcasted_iota(jnp.int32, (HALF, 128), 1)
        here = slice(half * HALF, (half + 1) * HALF)
        late[here, WIDTH : WIDTH + 128] = jnp.where(lanes < SLICES, block, own[here]).astype(BF16)
    late_sum.send(0)

    for index in range(len(grad_stages)):
        early_sum.fold(index)
        if index < early_sum.last():
            early_sum.send(index + 1)
        else:
            early_sum.gather(index)
        late_sum.fold(index)
        if index < late_sum.last():
            late_sum.send(index + 1)
        else:
            late_sum.gather(index)
    for index in reversed(range(len(grad_stages))):
        early_sum.settle(index)
        if index > 0:
            early_sum.gather(index - 1)
        else:
            gout_ref[...] = early_sum.total()[:, 0:WIDTH].astype(F32) * scale
            gwfx_ref[...] = early_sum.total()[:, WIDTH : 2 * WIDTH].astype(F32) * scale
        late_sum.settle(index)
        if index > 0:
            late_sum.gather(index - 1)
    gwx_ref[...] = late_sum.total()[:, 0:WIDTH].astype(F32) * scale
    extra = late_sum.total()[:, WIDTH : WIDTH + 128].astype(F32)
    extra = sum(extra[i * HEAD : (i + 1) * HEAD] for i in range(HEADS)) * scale
    gslice_ref[...] = extra[:, 0:SLICES]
    unit = (
        lax.broadcasted_iota(jnp.int32, (HEAD, HEAD), 0)
        == lax.broadcasted_iota(jnp.int32, (HEAD, HEAD), 1)
    ).astype(BF16)
    gtemp_ref[...] = pick3(extra, unit, mm_tn)[SLICES : SLICES + 1, :]


def body(devices, cells, counts, w_x, w_fx, w_slice, w_temp, w_qkv, w_out, cotangent):
    rows = cells.shape[0]
    token_stages = stages_of(devices, 2 * SLICES, 8)
    grad_stages = stages_of(devices, WIDTH, 16)
    scale = 1.0 / math.sqrt(rows * devices)
    vmem = pl.BlockSpec(memory_space=pltpu.VMEM)
    shape = jax.ShapeDtypeStruct
    outs = pl.pallas_call(
        functools.partial(layer_kernel, token_stages, grad_stages, scale),
        out_shape=(
            shape((rows, WIDTH), BF16),
            shape((rows, WIDTH), BF16),
            shape((WIDTH, WIDTH), F32),
            shape((WIDTH, WIDTH), F32),
            shape((HEAD, SLICES), F32),
            shape((1, HEAD), F32),
            shape((3, HEAD, HEAD), F32),
            shape((WIDTH, WIDTH), F32),
        ),
        in_specs=[pl.BlockSpec(memory_space=pltpu.SMEM)] + [vmem] * 8,
        out_specs=[vmem] * 8,
        scratch_shapes=[
            pltpu.VMEM((rows, WIDTH), BF16),
            pltpu.VMEM((rows, WIDTH), BF16),
            pltpu.VMEM((rows, WIDTH), BF16),
            pltpu.VMEM((rows, SPREAD), BF16),
            pltpu.VMEM((rows, SPREAD), F32),
            pltpu.VMEM((rows, SPREAD), F32),
            pltpu.VMEM((rows, SPREAD), F32),
            pltpu.VMEM((rows, 128), F32),
            pltpu.VMEM((rows, 128), F32),
            pltpu.VMEM((WIDTH, SPREAD), BF16),
            pltpu.VMEM((WIDTH, 128), BF16),
            pltpu.VMEM((128, WIDTH), BF16),
            pltpu.VMEM((2, 256, 2 * HALF + 128), F32),
            pltpu.VMEM((WIDTH, 2 * WIDTH), F32),
            pltpu.VMEM((WIDTH, WIDTH), F32),
            pltpu.VMEM((2, HALF, 256), F32),
            pltpu.VMEM((WIDTH, 128), F32),
            pltpu.VMEM((SPREAD, WIDTH), BF16),
            pltpu.VMEM((SPREAD, WIDTH), BF16),
        ]
        + Reduction.scratch(token_stages, WIDTH + 128, F32)
        + Reduction.scratch(grad_stages, 2 * WIDTH, BF16)
        + Reduction.scratch(grad_stages, WIDTH + 128, BF16),
        compiler_params=pltpu.CompilerParams(
            collective_id=0, has_side_effects=True, vmem_limit_bytes=44 * 1024 * 1024
        ),
    )(counts, cells, cotangent, w_x, w_fx, w_slice, w_temp.reshape(1, HEAD), w_qkv, w_out)
    result, gcells, gwx, gwfx, gslice, gtemp, gqkv, gout = outs
    return result, gcells, gwx, gwfx, gslice, gtemp.reshape(HEAD), gqkv, gout


def solution(mesh):
    placed = (
        P(("groups", "dom"), None),
        P(("groups", "dom")),
        P(),
        P(),
        P(),
        P(),
        P(),
        P(),
        P(("groups", "dom"), None),
    )
    return jax.shard_map(
        functools.partial(body, mesh.shape["dom"]),
        mesh=mesh,
        in_specs=placed,
        out_specs=(
            P(("groups", "dom"), None),
            P(("groups", "dom"), None),
            P("groups", None),
            P("groups", None),
            P("groups", None),
            P("groups"),
            P("groups", None, None),
            P("groups", None),
        ),
        check_vma=False,
    )
```

```python
import functools
import math

import jax
import jax.numpy as jnp
from jax import lax
from jax.experimental import pallas as pl
from jax.experimental.pallas import tpu as pltpu
from jax.sharding import PartitionSpec as P

HEAD = 32
SLICES = 64
HEADS = 8
WIDTH = HEAD * HEADS
SPREAD = SLICES * HEADS
HALF = WIDTH // 2
CHUNK = 256
F32 = jnp.float32
BF16 = jnp.bfloat16
MESH = pl.DeviceIdType.MESH


def mm(left, right):
    return jnp.dot(left, right, preferred_element_type=F32)


def mm_nt(left, right):
    return lax.dot_general(left, right, (((1,), (1,)), ((), ())), preferred_element_type=F32)


def mm_tn(left, right):
    return lax.dot_general(left, right, (((0,), (0,)), ((), ())), preferred_element_type=F32)


def split(value):
    high = value.astype(BF16)
    return high, (value - high.astype(F32)).astype(BF16)


def pick2(value, ones):
    high, low = split(value)
    return mm(high, ones) + mm(low, ones)


def pick3(value, ones, product=mm):
    high = value.astype(BF16)
    rest = value - high.astype(F32)
    middle, low = split(rest)
    return product(high, ones) + product(middle, ones) + product(low, ones)


def wide(left, right, product):
    left_high, left_low = split(left)
    right_high, right_low = split(right)
    return (
        product(left_high, right_high)
        + product(left_high, right_low)
        + product(left_low, right_high)
    )


def block_mask(shape, row_width, column_width):
    rows = lax.broadcasted_iota(jnp.int32, shape, 0)
    columns = lax.broadcasted_iota(jnp.int32, shape, 1)
    return (rows // row_width) == (columns // column_width)


def stages_of(devices, rows, tile):
    sizes, rest = [2], devices // 2
    while rest > 1:
        size = min(8, rest)
        sizes.append(size)
        rest //= size
    stages, stride = [], 1
    for size in sizes:
        scattered = rows % (size * tile) == 0
        stages.append((size, stride, rows, scattered))
        rows = rows // size if scattered else rows
        stride *= size
    return stages


def peers_of(stage):
    size, stride, _, _ = stage
    me = lax.axis_index("dom")
    place = lax.rem(lax.div(me, stride), size)
    others = []
    for step in range(1, size):
        there = lax.rem(place + step, size)
        others.append((there, me + (there - place) * stride))
    return place, others


class Reduction:
    @staticmethod
    def scratch(stages, columns, dtype):
        shapes = []
        for size, _, rows, scattered in stages:
            part = rows // size if scattered else rows
            shapes += [
                pltpu.VMEM((rows, columns), dtype),
                pltpu.VMEM((size, part, columns), dtype),
                pltpu.VMEM((rows, columns), dtype),
                pltpu.SemaphoreType.DMA((4, size)),
            ]
        return shapes

    def __init__(self, stages, refs):
        self.stages = stages
        self.levels = [refs[4 * i : 4 * i + 4] for i in range(len(stages))]

    def source(self):
        return self.levels[0][0]

    def total(self):
        return self.levels[0][2]

    def send(self, index):
        stage = self.stages[index]
        size, _, rows, scattered = stage
        source, received, _, sems = self.levels[index]
        place, others = peers_of(stage)
        part = rows // size if scattered else rows
        self.flying = []
        for step, (there, device) in enumerate(others):
            cut = source
            if scattered:
                cut = source.at[pl.ds(pl.multiple_of(there * part, part), part), :]
            copy = pltpu.make_async_remote_copy(
                src_ref=cut,
                dst_ref=received.at[place],
                send_sem=sems.at[0, step],
                recv_sem=sems.at[1, step],
                device_id={"dom": device},
                device_id_type=MESH,
            )
            copy.start()
            self.flying.append(copy)
        if scattered:
            received[place] = source[pl.ds(pl.multiple_of(place * part, part), part), :]
        else:
            received[place] = source[...]

    def fold(self, index):
        size, _, rows, scattered = self.stages[index]
        source, received, gathered, _ = self.levels[index]
        for copy in self.flying:
            copy.wait()
        total = received[0].astype(F32)
        for slot in range(1, size):
            total = total + received[slot].astype(F32)
        total = total.astype(source.dtype)
        if index + 1 < len(self.stages):
            self.levels[index + 1][0][...] = total
        else:
            self.place(index, total)

    def place(self, index, value):
        size, _, rows, scattered = self.stages[index]
        gathered = self.levels[index][2]
        if scattered:
            part = rows // size
            place, _ = peers_of(self.stages[index])
            gathered[pl.ds(pl.multiple_of(place * part, part), part), :] = value
        else:
            gathered[...] = value

    def gather(self, index):
        stage = self.stages[index]
        size, _, rows, scattered = stage
        gathered, sems = self.levels[index][2:]
        self.flying = []
        if not scattered:
            return
        part = rows // size
        place, others = peers_of(stage)
        mine = gathered.at[pl.ds(pl.multiple_of(place * part, part), part), :]
        for step, (_, device) in enumerate(others):
            copy = pltpu.make_async_remote_copy(
                src_ref=mine,
                dst_ref=mine,
                send_sem=sems.at[2, step],
                recv_sem=sems.at[3, step],
                device_id={"dom": device},
                device_id_type=MESH,
            )
            copy.start()
            self.flying.append(copy)

    def settle(self, index):
        for copy in self.flying:
            copy.wait()
        if index > 0:
            self.place(index - 1, self.levels[index][2][...])

    def last(self):
        return len(self.stages) - 1


def layer_kernel(
    token_stages,
    grad_stages,
    scale,
    counts_hbm,
    cells_hbm,
    cot_hbm,
    wx_hbm,
    wfx_hbm,
    wslice_hbm,
    wtemp_hbm,
    wqkv_hbm,
    wout_hbm,
    result_hbm,
    gcells_hbm,
    gwx_hbm,
    gwfx_hbm,
    gslice_hbm,
    gtemp_hbm,
    gqkv_hbm,
    gout_hbm,
    counts_ref,
    cells_ref,
    cot_ref,
    wx_ref,
    wfx_ref,
    wslice_ref,
    wtemp_ref,
    wqkv_ref,
    wout_ref,
    result_ref,
    gcells_ref,
    gwx_ref,
    gwfx_ref,
    gslice_ref,
    gtemp_ref,
    gqkv_ref,
    gout_ref,
    in_sems,
    out_sems,
    proj_ref,
    pair_ref,
    weight_ref,
    prob_ref,
    slope_ref,
    scaled_ref,
    inverse_ref,
    sigmoid_ref,
    cells_t,
    cot_t,
    proj_t,
    hidden_ref,
    dfeat_ref,
    dproj_ref,
    dlogit_ref,
    dtemp_ref,
    slice_bd,
    temp_bd,
    temp_row,
    same_head,
    maps_ref,
    acc_tokens,
    both_bd,
    *sum_refs,
):
    rows = cells_ref.shape[0]
    chunks = rows // CHUNK
    middle = chunks // 2
    levels = 4 * len(token_stages)
    levels_g = 4 * len(grad_stages)
    token_sum = Reduction(token_stages, sum_refs[:levels])
    early_sum, late_sum, last_sum = [
        Reduction(grad_stages, sum_refs[levels + i * levels_g : levels + (i + 1) * levels_g])
        for i in range(3)
    ]

    pairs = (
        (wslice_hbm, wslice_ref),
        (wtemp_hbm, wtemp_ref),
        (cells_hbm, cells_ref),
        (wx_hbm, wx_ref),
        (counts_hbm, counts_ref),
        (wfx_hbm, wfx_ref),
        (wout_hbm, wout_ref),
        (cot_hbm, cot_ref),
        (wqkv_hbm, wqkv_ref),
    )
    incoming = [
        pltpu.make_async_copy(there, here, in_sems.at[i]) for i, (there, here) in enumerate(pairs)
    ]
    for copy in incoming:
        copy.start()
    barrier = pltpu.get_barrier_semaphore()
    greeted = 0
    for stage in token_stages:
        for _, device in peers_of(stage)[1]:
            pl.semaphore_signal(barrier, inc=1, device_id={"dom": device}, device_id_type=MESH)
            greeted += 1
    outgoing = []

    def put(source, target):
        copy = pltpu.make_async_copy(source, target, out_sems.at[len(outgoing)])
        copy.start()
        outgoing.append(copy)

    repeat32 = (
        (lax.broadcasted_iota(jnp.int32, (HEAD, HALF), 1) % HEAD)
        == lax.broadcasted_iota(jnp.int32, (HEAD, HALF), 0)
    ).astype(BF16)
    repeat64 = (
        (lax.broadcasted_iota(jnp.int32, (SLICES, 256), 1) % SLICES)
        == lax.broadcasted_iota(jnp.int32, (SLICES, 256), 0)
    ).astype(BF16)
    lane_head = lax.broadcasted_iota(jnp.int32, (256, 128), 1)
    row_head = lax.broadcasted_iota(jnp.int32, (256, 128), 0) // SLICES
    gather_heads = [(row_head + 4 * half == lane_head).astype(BF16) for half in range(2)]
    spread_lane = lax.broadcasted_iota(jnp.int32, (128, 256), 1) // SLICES
    spread_row = lax.broadcasted_iota(jnp.int32, (128, 256), 0)
    spread_heads = [(spread_lane + 4 * half == spread_row).astype(BF16) for half in range(2)]
    half_diag = block_mask((256, HALF), SLICES, HEAD)
    same_head[...] = block_mask((256, 256), SLICES, SLICES).astype(BF16)

    incoming[0].wait()
    incoming[1].wait()
    tall = mm_tn(repeat32, wslice_ref[...]).astype(BF16)
    slice_bd[...] = jnp.where(
        block_mask((HALF, 256), HEAD, SLICES), mm(tall, repeat64), 0.0
    ).astype(BF16)
    temp_rows = jnp.broadcast_to(wtemp_ref[...], (128, HEAD))
    column = mm_nt(repeat32.T, temp_rows)
    line = mm(temp_rows, repeat32)
    for half in range(2):
        place = slice(half * HALF, (half + 1) * HALF)
        lanes = lax.broadcasted_iota(jnp.int32, (HALF, 128), 1)
        heads = lax.broadcasted_iota(jnp.int32, (HALF, 128), 0) // HEAD + 4 * half
        temp_bd[place, :] = jnp.where(lanes == heads, column, 0.0).astype(BF16)
        heads = lax.broadcasted_iota(jnp.int32, (128, HALF), 1) // HEAD + 4 * half
        here = lax.broadcasted_iota(jnp.int32, (128, HALF), 0)
        temp_row[:, place] = jnp.where(here == heads, line, 0.0).astype(BF16)
    acc_tokens[...] = jnp.zeros_like(acc_tokens)
    for copy in incoming[2:]:
        copy.wait()
    count = counts_ref[0]

    def cut(index):
        return pl.ds(pl.multiple_of(index * CHUNK, CHUNK), CHUNK)

    def forward(index, carry):
        part = cut(index)
        cells = cells_ref[part, :]
        projected = mm(cells, wx_ref[...]).astype(BF16)
        features = mm(cells, wfx_ref[...]).astype(BF16)
        d_hidden = mm_nt(cot_ref[part, :], wout_ref[...]).astype(BF16)
        temp_lin = mm(projected, temp_bd[...])
        away = jnp.exp(-jnp.abs(temp_lin))
        temper = 0.5 + (jnp.maximum(temp_lin, 0.0) + jnp.log(1.0 + away))
        inverse = 1.0 / temper
        sigmoid = jnp.where(temp_lin >= 0.0, 1.0, away) / (1.0 + away)
        proj_ref[part, :] = projected
        inverse_ref[part, :] = inverse
        sigmoid_ref[part, :] = sigmoid
        inverse_high, inverse_low = split(inverse)
        place = lax.broadcasted_iota(jnp.int32, (CHUNK, 1), 0) + index * CHUNK
        live = (place < count).astype(F32)
        for half in range(2):
            lanes = slice(half * HALF, (half + 1) * HALF)
            span = slice(half * 256, (half + 1) * 256)
            bent = jnp.tanh(mm(projected[:, lanes], slice_bd[...]) / 10.0)
            cool = mm(inverse_high, spread_heads[half]) + mm(inverse_low, spread_heads[half])
            scaled = (10.0 * bent) * cool
            powers = jnp.exp(scaled)
            probs = powers * (live / pick2(powers, same_head[...]))
            weights = probs.astype(BF16)
            weight_ref[part, span] = weights
            prob_ref[part, span] = probs
            slope_ref[part, span] = (1.0 - bent * bent) * cool
            scaled_ref[part, span] = scaled
            pair = jnp.concatenate([d_hidden[:, lanes], features[:, lanes]], axis=1)
            pair_ref[part, span] = pair
            right = jnp.concatenate([pair, jnp.ones((CHUNK, 128), BF16)], axis=1)
            acc_tokens[half] += mm_tn(weights, right)
        return carry

    lax.fori_loop(0, chunks, forward, 0)

    payload = token_sum.source()
    lane = lax.broadcasted_iota(jnp.int32, (SLICES, 128), 1)
    totals = jnp.zeros((SLICES, 128), F32)
    for half in range(2):
        lanes = slice(half * HALF, (half + 1) * HALF)
        dmix = jnp.where(half_diag, acc_tokens[half, :, 0:HALF], 0.0)
        numer = jnp.where(half_diag, acc_tokens[half, :, HALF : 2 * HALF], 0.0)
        payload[0:SLICES, lanes] = sum(numer[i * 64 : i * 64 + 64] for i in range(4))
        payload[SLICES : 2 * SLICES, lanes] = sum(dmix[i * 64 : i * 64 + 64] for i in range(4))
        for i in range(4):
            block = acc_tokens[half, i * 64 : i * 64 + 64, 2 * HALF : 2 * HALF + 128]
            totals = totals + jnp.where(lane == half * 4 + i, block, 0.0)
    payload[0:SLICES, WIDTH : WIDTH + 128] = totals
    payload[SLICES : 2 * SLICES, WIDTH : WIDTH + 128] = jnp.zeros((SLICES, 128), F32)

    pl.semaphore_wait(barrier, greeted)
    diag_square = block_mask((WIDTH, WIDTH), HEAD, HEAD)

    def prepare_maps():
        for k in range(3):
            square = mm(mm_tn(repeat32, wqkv_ref[k]).astype(BF16), repeat32)
            square = jnp.concatenate([square, square], axis=0)
            square = jnp.concatenate([square, square], axis=1)
            maps_ref[k] = jnp.where(diag_square, square, 0.0).astype(BF16)

    def turn(source, target):
        for index in range(chunks):
            part = slice(index * CHUNK, (index + 1) * CHUNK)
            target[:, part] = source[part, :].T

    fillers = [
        prepare_maps,
        functools.partial(turn, cells_ref, cells_t),
        functools.partial(turn, cot_ref, cot_t),
        functools.partial(turn, proj_ref, proj_t),
    ]
    for index in range(len(token_stages)):
        token_sum.send(index)
        if fillers:
            fillers.pop(0)()
        token_sum.fold(index)
    for index in reversed(range(len(token_stages))):
        token_sum.gather(index)
        if fillers:
            fillers.pop(0)()
        token_sum.settle(index)
    for filler in fillers:
        filler()

    total = token_sum.total()
    numerators = total[0:SLICES, 0:WIDTH]
    d_mixed = total[SLICES : 2 * SLICES, 0:WIDTH]
    spread32 = block_mask((128, WIDTH), 1, HEAD).astype(BF16)
    denominators = pick3(total[0:SLICES, WIDTH : WIDTH + 128], spread32) + 1e-05
    tokens = numerators / denominators
    queries, key_rows, value_rows = [pick2(tokens, maps_ref[k]) for k in range(3)]

    def expand(value):
        return jnp.where(half_diag, jnp.concatenate([value] * 4, axis=0), 0.0)

    def contract(value):
        value = jnp.where(half_diag, value, 0.0)
        return sum(value[i * SLICES : (i + 1) * SLICES] for i in range(4))

    root = 1.0 / math.sqrt(HEAD)
    halves = [slice(half * HALF, (half + 1) * HALF) for half in range(2)]
    keys_bd = [expand(key_rows[:, lanes]) for lanes in halves]
    values_bd = [expand(value_rows[:, lanes]) for lanes in halves]
    d_attention = [wide(d_mixed[:, halves[i]], values_bd[i], mm_nt) for i in range(2)]
    bent = [
        jnp.tanh(wide(queries[:, halves[i]], keys_bd[i], mm_nt) * root / 10.0) for i in range(2)
    ]
    powers = [jnp.exp(10.0 * value) for value in bent]
    attention = [value / pick2(value, same_head[...]) for value in powers]
    for i in range(2):
        mixed = wide(attention[i], values_bd[i], mm)
        both_bd[i, :, 0:HALF] = expand(mixed).astype(BF16)
    shared = [attention[i] * d_attention[i] for i in range(2)]
    shared = [shared[i] - attention[i] * pick2(shared[i], same_head[...]) for i in range(2)]
    d_scores = [shared[i] * (1.0 - bent[i] * bent[i]) * root for i in range(2)]
    d_queries = jnp.concatenate([wide(d_scores[i], keys_bd[i], mm) for i in range(2)], axis=1)
    d_keys = jnp.concatenate(
        [contract(wide(d_scores[i], queries[:, halves[i]], mm_tn)) for i in range(2)], axis=1
    )
    d_values = jnp.concatenate(
        [contract(wide(attention[i], d_mixed[:, halves[i]], mm_tn)) for i in range(2)], axis=1
    )
    d_maps = (d_queries, d_keys, d_values)

    def pick_back(value, weight):
        high, low = split(value)
        return mm_nt(high, weight) + mm_nt(low, weight)

    d_tokens = sum(pick_back(d_maps[k], maps_ref[k]) for k in range(3))
    d_numer = d_tokens / denominators
    away = d_numer * tokens
    d_denom = []
    for i in range(2):
        both_bd[i, :, HALF : 2 * HALF] = expand(d_numer[:, halves[i]]).astype(BF16)
        high, low = split(expand(away[:, halves[i]]))
        ones = jnp.ones((128, HALF), BF16)
        d_denom.append(-(mm_nt(ones, high) + mm_nt(ones, low))[0:1, :])

    def early(index, carry):
        part = cut(index)
        for half in range(2):
            lanes = slice(half * HALF, (half + 1) * HALF)
            made = mm(weight_ref[part, half * 256 : (half + 1) * 256], both_bd[half]).astype(BF16)
            hidden_ref[part, lanes] = made[:, 0:HALF]
            dfeat_ref[part, lanes] = made[:, HALF : 2 * HALF]
        return carry

    lax.fori_loop(0, chunks, early, 0)
    source = early_sum.source()
    source[:, 0:WIDTH] = mm(cot_t[...], hidden_ref[...]).astype(BF16)
    source[:, WIDTH : 2 * WIDTH] = mm(cells_t[...], dfeat_ref[...]).astype(BF16)

    def backward(half, index, carry):
        part = cut(index)
        lanes = slice(half * HALF, (half + 1) * HALF)
        span = slice(half * 256, (half + 1) * 256)
        d_weights = mm_nt(pair_ref[part, span], both_bd[half]) + d_denom[half]
        probs = prob_ref[part, span]
        shared = probs * d_weights
        shared = shared - probs * pick2(shared, same_head[...])
        d_logits = (shared * slope_ref[part, span]).astype(BF16)
        d_temper = -pick2(shared * scaled_ref[part, span], gather_heads[half])
        d_temp = (d_temper * inverse_ref[part, :] * sigmoid_ref[part, :]).astype(BF16)
        dlogit_ref[part, :] = d_logits
        dtemp_ref[part, :] = d_temp
        dproj_ref[part, lanes] = (
            mm_nt(d_logits, slice_bd[...]) + mm(d_temp, temp_row[:, lanes])
        ).astype(BF16)
        return carry

    def fill(half, target):
        lanes = slice(half * HALF, (half + 1) * HALF)
        block = mm(proj_t[lanes, :], dlogit_ref[...])
        block = jnp.where(block_mask((HALF, 256), HEAD, SLICES), block, 0.0)
        block = block[:, 0:128] + block[:, 128:256]
        block = block + pltpu.roll(block, 64, 1)
        here = lax.broadcasted_iota(jnp.int32, (HALF, 128), 1)
        heads = lax.broadcasted_iota(jnp.int32, (HALF, 128), 0) // HEAD + 4 * half
        own = jnp.where(here == heads, mm(proj_t[lanes, :], dtemp_ref[...]), 0.0)
        own = jnp.sum(own, axis=1, keepdims=True)
        target[:, 0:128] = mm(cells_t[...], dproj_ref[:, lanes]).astype(BF16)
        target[0:HALF, 128:256] = jnp.where(here < SLICES, block, own).astype(BF16)
        target[HALF:WIDTH, 128:256] = jnp.zeros((WIDTH - HALF, 128), BF16)

    def results(index, carry):
        part = cut(index)
        result_ref[part, :] = mm(hidden_ref[part, :], wout_ref[...]).astype(BF16)
        return carry

    def cell_grads(index, carry):
        part = cut(index)
        gcells_ref[part, :] = (
            mm_nt(dproj_ref[part, :], wx_ref[...]) + mm_nt(dfeat_ref[part, :], wfx_ref[...])
        ).astype(BF16)
        return carry

    def steps(reduction):
        for index in range(len(grad_stages)):
            reduction.send(index)
            yield
            reduction.fold(index)
        for index in reversed(range(len(grad_stages))):
            reduction.gather(index)
            yield
            reduction.settle(index)

    early_steps, late_steps, last_steps = steps(early_sum), steps(late_sum), steps(last_sum)
    next(early_steps)
    lax.fori_loop(0, middle, functools.partial(backward, 0), 0)
    next(early_steps)
    lax.fori_loop(middle, chunks, functools.partial(backward, 0), 0)
    fill(0, late_sum.source())
    next(late_steps)
    next(early_steps)
    lax.fori_loop(0, middle, functools.partial(backward, 1), 0)
    next(late_steps)
    next(early_steps)
    lax.fori_loop(middle, chunks, functools.partial(backward, 1), 0)
    fill(1, last_sum.source())
    next(last_steps)
    next(late_steps)
    lax.fori_loop(0, chunks, cell_grads, 0)
    put(gcells_ref, gcells_hbm)
    next(last_steps)
    for _ in early_steps:
        pass
    lax.fori_loop(0, chunks, results, 0)
    put(result_ref, result_hbm)
    gwfx_ref[...] = early_sum.total()[:, WIDTH : 2 * WIDTH].astype(F32) * scale
    put(gwfx_ref, gwfx_hbm)
    gout_ref[...] = early_sum.total()[:, 0:WIDTH].astype(F32).T * scale
    put(gout_ref, gout_hbm)
    next(late_steps)
    for k in range(3):
        square = jnp.where(diag_square, wide(tokens, d_maps[k], mm_tn), 0.0)
        strip = sum(square[i * HEAD : (i + 1) * HEAD] for i in range(HEADS))
        strip = strip[:, 0:HALF] + strip[:, HALF:WIDTH]
        gqkv_ref[k] = pick2(strip, repeat32.T) * scale
    put(gqkv_ref, gqkv_hbm)
    next(last_steps)
    for _ in late_steps:
        pass
    gwx_ref[:, 0:HALF] = late_sum.total()[:, 0:HALF].astype(F32) * scale
    for _ in last_steps:
        pass
    gwx_ref[:, HALF:WIDTH] = last_sum.total()[:, 0:HALF].astype(F32) * scale
    put(gwx_ref, gwx_hbm)
    extra = sum(
        reduction.total()[0:HALF, 128:256].astype(F32) for reduction in (late_sum, last_sum)
    )
    extra = sum(extra[i * HEAD : (i + 1) * HEAD] for i in range(4)) * scale
    gslice_ref[...] = extra[:, 0:SLICES]
    put(gslice_ref, gslice_hbm)
    unit = (
        lax.broadcasted_iota(jnp.int32, (HEAD, HEAD), 0)
        == lax.broadcasted_iota(jnp.int32, (HEAD, HEAD), 1)
    ).astype(BF16)
    gtemp_ref[...] = pick3(extra, unit, mm_tn)[SLICES : SLICES + 1, :]
    put(gtemp_ref, gtemp_hbm)
    for copy in outgoing:
        copy.wait()


def hand_over(*refs):
    count = (len(refs) - 1) // 2
    copies = [
        pltpu.make_async_copy(refs[i], refs[count + i], refs[-1].at[i]) for i in range(count)
    ]
    for copy in copies:
        copy.start()
    for copy in copies:
        copy.wait()


def body(devices, cells, counts, w_x, w_fx, w_slice, w_temp, w_qkv, w_out, cotangent):
    rows = cells.shape[0]
    token_stages = stages_of(devices, 2 * SLICES, 8)
    grad_stages = stages_of(devices, WIDTH, 16)
    scale = 1.0 / math.sqrt(rows * devices)
    anywhere = pl.BlockSpec(memory_space=pl.ANY)
    vmem = pltpu.VMEM
    out_shapes = [
        ((rows, WIDTH), BF16),
        ((rows, WIDTH), BF16),
        ((WIDTH, WIDTH), F32),
        ((WIDTH, WIDTH), F32),
        ((HEAD, SLICES), F32),
        ((1, HEAD), F32),
        ((3, HEAD, HEAD), F32),
        ((WIDTH, WIDTH), F32),
    ]
    out_shape = tuple(jax.ShapeDtypeStruct(*one) for one in out_shapes)
    outs = pl.pallas_call(
        functools.partial(layer_kernel, token_stages, grad_stages, scale),
        out_shape=out_shape,
        in_specs=[anywhere] * 9,
        out_specs=[anywhere] * 8,
        scratch_shapes=[
            pltpu.SMEM((1,), jnp.int32),
            vmem((rows, WIDTH), BF16),
            vmem((rows, WIDTH), BF16),
            vmem((WIDTH, WIDTH), BF16),
            vmem((WIDTH, WIDTH), BF16),
            vmem((HEAD, SLICES), BF16),
            vmem((1, HEAD), BF16),
            vmem((3, HEAD, HEAD), BF16),
            vmem((WIDTH, WIDTH), BF16),
        ]
        + [vmem(*one) for one in out_shapes]
        + [
            pltpu.SemaphoreType.DMA((9,)),
            pltpu.SemaphoreType.DMA((8,)),
            vmem((rows, WIDTH), BF16),
            vmem((rows, SPREAD), BF16),
            vmem((rows, SPREAD), BF16),
            vmem((rows, SPREAD), F32),
            vmem((rows, SPREAD), F32),
            vmem((rows, SPREAD), F32),
            vmem((rows, 128), F32),
            vmem((rows, 128), F32),
            vmem((WIDTH, rows), BF16),
            vmem((WIDTH, rows), BF16),
            vmem((WIDTH, rows), BF16),
            vmem((rows, WIDTH), BF16),
            vmem((rows, WIDTH), BF16),
            vmem((rows, WIDTH), BF16),
            vmem((rows, 256), BF16),
            vmem((rows, 128), BF16),
            vmem((HALF, 256), BF16),
            vmem((WIDTH, 128), BF16),
            vmem((128, WIDTH), BF16),
            vmem((256, 256), BF16),
            vmem((3, WIDTH, WIDTH), BF16),
            vmem((2, 256, 2 * HALF + 128), F32),
            vmem((2, 256, 2 * HALF), BF16),
        ]
        + Reduction.scratch(token_stages, WIDTH + 128, F32)
        + Reduction.scratch(grad_stages, 2 * WIDTH, BF16)
        + Reduction.scratch(grad_stages, 256, BF16)
        + Reduction.scratch(grad_stages, 256, BF16),
        compiler_params=pltpu.CompilerParams(
            collective_id=0, has_side_effects=True, vmem_limit_bytes=60 * 1024 * 1024
        ),
    )(counts, cells, cotangent, w_x, w_fx, w_slice, w_temp.reshape(1, HEAD), w_qkv, w_out)
    outs = pl.pallas_call(
        hand_over,
        out_shape=out_shape,
        in_specs=[anywhere] * 8,
        out_specs=[anywhere] * 8,
        scratch_shapes=[pltpu.SemaphoreType.DMA((8,))],
        compiler_params=pltpu.CompilerParams(vmem_limit_bytes=60 * 1024 * 1024),
    )(*outs)
    result, gcells, gwx, gwfx, gslice, gtemp, gqkv, gout = outs
    return result, gcells, gwx, gwfx, gslice, gtemp.reshape(HEAD), gqkv, gout


def solution(mesh):
    placed = (
        P(("groups", "dom"), None),
        P(("groups", "dom")),
        P(),
        P(),
        P(),
        P(),
        P(),
        P(),
        P(("groups", "dom"), None),
    )
    return jax.shard_map(
        functools.partial(body, mesh.shape["dom"]),
        mesh=mesh,
        in_specs=placed,
        out_specs=(
            P(("groups", "dom"), None),
            P(("groups", "dom"), None),
            P("groups", None),
            P("groups", None),
            P("groups", None),
            P("groups"),
            P("groups", None, None),
            P("groups", None),
        ),
        check_vma=False,
    )
```

```python
import functools
import math

import jax
import jax.numpy as jnp
from jax import lax
from jax.experimental import pallas as pl
from jax.experimental.pallas import tpu as pltpu
from jax.sharding import PartitionSpec as P

HEAD = 32
SLICES = 64
HEADS = 8
WIDTH = HEAD * HEADS
SPREAD = SLICES * HEADS
HALF = WIDTH // 2
CHUNK = 256
F32 = jnp.float32
BF16 = jnp.bfloat16
MESH = pl.DeviceIdType.MESH


def mm(left, right):
    return jnp.dot(left, right, preferred_element_type=F32)


def mm_nt(left, right):
    return lax.dot_general(left, right, (((1,), (1,)), ((), ())), preferred_element_type=F32)


def mm_tn(left, right):
    return lax.dot_general(left, right, (((0,), (0,)), ((), ())), preferred_element_type=F32)


def split(value):
    high = value.astype(BF16)
    return high, (value - high.astype(F32)).astype(BF16)


def pick2(value, ones):
    high, low = split(value)
    return mm(high, ones) + mm(low, ones)


def pick3(value, ones, product=mm):
    high = value.astype(BF16)
    rest = value - high.astype(F32)
    middle, low = split(rest)
    return product(high, ones) + product(middle, ones) + product(low, ones)


def wide(left, right, product):
    left_high, left_low = split(left)
    right_high, right_low = split(right)
    return (
        product(left_high, right_high)
        + product(left_high, right_low)
        + product(left_low, right_high)
    )


def block_mask(shape, row_width, column_width):
    rows = lax.broadcasted_iota(jnp.int32, shape, 0)
    columns = lax.broadcasted_iota(jnp.int32, shape, 1)
    return (rows // row_width) == (columns // column_width)


def stages_of(devices, rows, tile):
    sizes, rest = [2], devices // 2
    while rest > 1:
        size = min(8, rest)
        sizes.append(size)
        rest //= size
    stages, stride = [], 1
    for size in sizes:
        scattered = rows % (size * tile) == 0
        stages.append((size, stride, rows, scattered))
        rows = rows // size if scattered else rows
        stride *= size
    return stages


def peers_of(stage):
    size, stride, _, _ = stage
    me = lax.axis_index("dom")
    place = lax.rem(lax.div(me, stride), size)
    others = []
    for step in range(1, size):
        there = lax.rem(place + step, size)
        others.append((there, me + (there - place) * stride))
    return place, others


class Reduction:
    @staticmethod
    def scratch(stages, columns, dtype):
        shapes = []
        for size, _, rows, scattered in stages:
            part = rows // size if scattered else rows
            shapes += [
                pltpu.VMEM((rows, columns), dtype),
                pltpu.VMEM((size, part, columns), dtype),
                pltpu.VMEM((rows, columns), dtype),
                pltpu.SemaphoreType.DMA((4, size)),
            ]
        return shapes

    def __init__(self, stages, refs):
        self.stages = stages
        self.levels = [refs[4 * i : 4 * i + 4] for i in range(len(stages))]

    def source(self):
        return self.levels[0][0]

    def total(self):
        return self.levels[0][2]

    def send(self, index):
        stage = self.stages[index]
        size, _, rows, scattered = stage
        source, received, _, sems = self.levels[index]
        place, others = peers_of(stage)
        part = rows // size if scattered else rows
        self.flying = []
        for step, (there, device) in enumerate(others):
            cut = source
            if scattered:
                cut = source.at[pl.ds(pl.multiple_of(there * part, part), part), :]
            copy = pltpu.make_async_remote_copy(
                src_ref=cut,
                dst_ref=received.at[place],
                send_sem=sems.at[0, step],
                recv_sem=sems.at[1, step],
                device_id={"dom": device},
                device_id_type=MESH,
            )
            copy.start()
            self.flying.append(copy)
        if scattered:
            received[place] = source[pl.ds(pl.multiple_of(place * part, part), part), :]
        else:
            received[place] = source[...]

    def fold(self, index):
        size, _, rows, scattered = self.stages[index]
        source, received, gathered, _ = self.levels[index]
        for copy in self.flying:
            copy.wait()
        total = received[0].astype(F32)
        for slot in range(1, size):
            total = total + received[slot].astype(F32)
        total = total.astype(source.dtype)
        if index + 1 < len(self.stages):
            self.levels[index + 1][0][...] = total
        else:
            self.place(index, total)

    def place(self, index, value):
        size, _, rows, scattered = self.stages[index]
        gathered = self.levels[index][2]
        if scattered:
            part = rows // size
            place, _ = peers_of(self.stages[index])
            gathered[pl.ds(pl.multiple_of(place * part, part), part), :] = value
        else:
            gathered[...] = value

    def gather(self, index):
        stage = self.stages[index]
        size, _, rows, scattered = stage
        gathered, sems = self.levels[index][2:]
        self.flying = []
        if not scattered:
            return
        part = rows // size
        place, others = peers_of(stage)
        mine = gathered.at[pl.ds(pl.multiple_of(place * part, part), part), :]
        for step, (_, device) in enumerate(others):
            copy = pltpu.make_async_remote_copy(
                src_ref=mine,
                dst_ref=mine,
                send_sem=sems.at[2, step],
                recv_sem=sems.at[3, step],
                device_id={"dom": device},
                device_id_type=MESH,
            )
            copy.start()
            self.flying.append(copy)

    def settle(self, index):
        for copy in self.flying:
            copy.wait()
        if index > 0:
            self.place(index - 1, self.levels[index][2][...])

    def last(self):
        return len(self.stages) - 1


def layer_kernel(
    token_stages,
    grad_stages,
    scale,
    counts_hbm,
    cells_hbm,
    cot_hbm,
    wx_hbm,
    wfx_hbm,
    wslice_hbm,
    wtemp_hbm,
    wqkv_hbm,
    wout_hbm,
    result_hbm,
    gcells_hbm,
    gwx_hbm,
    gwfx_hbm,
    gslice_hbm,
    gtemp_hbm,
    gqkv_hbm,
    gout_hbm,
    counts_ref,
    cells_ref,
    cot_ref,
    wx_ref,
    wfx_ref,
    wslice_ref,
    wtemp_ref,
    wqkv_ref,
    wout_ref,
    result_ref,
    gcells_ref,
    gwx_ref,
    gwfx_ref,
    gslice_ref,
    gtemp_ref,
    gqkv_ref,
    gout_ref,
    in_sems,
    out_sems,
    proj_ref,
    pair_ref,
    weight_ref,
    prob_ref,
    slope_ref,
    scaled_ref,
    inverse_ref,
    sigmoid_ref,
    cells_t,
    cot_t,
    proj_t,
    hidden_ref,
    dfeat_ref,
    dproj_ref,
    dlogit_ref,
    dtemp_ref,
    slice_bd,
    temp_bd,
    temp_row,
    same_head,
    maps_ref,
    acc_tokens,
    both_bd,
    both_t,
    slice_t,
    wout_t,
    wx_t,
    wfx_t,
    *sum_refs,
):
    rows = cells_ref.shape[0]
    chunks = rows // CHUNK
    middle = chunks // 2
    levels = 4 * len(token_stages)
    levels_g = 4 * len(grad_stages)
    token_sum = Reduction(token_stages, sum_refs[:levels])
    early_sum, late_sum, last_sum = [
        Reduction(grad_stages, sum_refs[levels + i * levels_g : levels + (i + 1) * levels_g])
        for i in range(3)
    ]

    pairs = (
        (wslice_hbm, wslice_ref),
        (wtemp_hbm, wtemp_ref),
        (cells_hbm, cells_ref),
        (wx_hbm, wx_ref),
        (counts_hbm, counts_ref),
        (wfx_hbm, wfx_ref),
        (wout_hbm, wout_ref),
        (cot_hbm, cot_ref),
        (wqkv_hbm, wqkv_ref),
    )
    incoming = [
        pltpu.make_async_copy(there, here, in_sems.at[i]) for i, (there, here) in enumerate(pairs)
    ]
    for copy in incoming:
        copy.start()
    barrier = pltpu.get_barrier_semaphore()
    greeted = 0
    for stage in token_stages:
        for _, device in peers_of(stage)[1]:
            pl.semaphore_signal(barrier, inc=1, device_id={"dom": device}, device_id_type=MESH)
            greeted += 1
    outgoing = []

    def put(source, target):
        copy = pltpu.make_async_copy(source, target, out_sems.at[len(outgoing)])
        copy.start()
        outgoing.append(copy)

    repeat32 = (
        (lax.broadcasted_iota(jnp.int32, (HEAD, HALF), 1) % HEAD)
        == lax.broadcasted_iota(jnp.int32, (HEAD, HALF), 0)
    ).astype(BF16)
    repeat64 = (
        (lax.broadcasted_iota(jnp.int32, (SLICES, 256), 1) % SLICES)
        == lax.broadcasted_iota(jnp.int32, (SLICES, 256), 0)
    ).astype(BF16)
    lane_head = lax.broadcasted_iota(jnp.int32, (256, 128), 1)
    row_head = lax.broadcasted_iota(jnp.int32, (256, 128), 0) // SLICES
    gather_heads = [(row_head + 4 * half == lane_head).astype(BF16) for half in range(2)]
    spread_lane = lax.broadcasted_iota(jnp.int32, (128, 256), 1) // SLICES
    spread_row = lax.broadcasted_iota(jnp.int32, (128, 256), 0)
    spread_heads = [(spread_lane + 4 * half == spread_row).astype(BF16) for half in range(2)]
    half_diag = block_mask((256, HALF), SLICES, HEAD)
    same_head[...] = block_mask((256, 256), SLICES, SLICES).astype(BF16)

    incoming[0].wait()
    incoming[1].wait()
    tall = mm_tn(repeat32, wslice_ref[...]).astype(BF16)
    slice_bd[...] = jnp.where(
        block_mask((HALF, 256), HEAD, SLICES), mm(tall, repeat64), 0.0
    ).astype(BF16)
    temp_rows = jnp.broadcast_to(wtemp_ref[...], (128, HEAD))
    column = mm_nt(repeat32.T, temp_rows)
    line = mm(temp_rows, repeat32)
    for half in range(2):
        place = slice(half * HALF, (half + 1) * HALF)
        lanes = lax.broadcasted_iota(jnp.int32, (HALF, 128), 1)
        heads = lax.broadcasted_iota(jnp.int32, (HALF, 128), 0) // HEAD + 4 * half
        temp_bd[place, :] = jnp.where(lanes == heads, column, 0.0).astype(BF16)
        heads = lax.broadcasted_iota(jnp.int32, (128, HALF), 1) // HEAD + 4 * half
        here = lax.broadcasted_iota(jnp.int32, (128, HALF), 0)
        temp_row[:, place] = jnp.where(here == heads, line, 0.0).astype(BF16)
    acc_tokens[...] = jnp.zeros_like(acc_tokens)
    for copy in incoming[2:]:
        copy.wait()
    wout_t[...] = wout_ref[...].T
    count = counts_ref[0]

    def cut(index):
        return pl.ds(pl.multiple_of(index * CHUNK, CHUNK), CHUNK)

    def forward(index, carry):
        part = cut(index)
        cells = cells_ref[part, :]
        projected = mm(cells, wx_ref[...]).astype(BF16)
        features = mm(cells, wfx_ref[...]).astype(BF16)
        d_hidden = mm(cot_ref[part, :], wout_t[...]).astype(BF16)
        temp_lin = mm(projected, temp_bd[...])
        away = jnp.exp(-jnp.abs(temp_lin))
        temper = 0.5 + (jnp.maximum(temp_lin, 0.0) + jnp.log(1.0 + away))
        inverse = 1.0 / temper
        sigmoid = jnp.where(temp_lin >= 0.0, 1.0, away) / (1.0 + away)
        proj_ref[part, :] = projected
        inverse_ref[part, :] = inverse
        sigmoid_ref[part, :] = sigmoid
        inverse_high, inverse_low = split(inverse)
        place = lax.broadcasted_iota(jnp.int32, (CHUNK, 1), 0) + index * CHUNK
        live = (place < count).astype(F32)
        for half in range(2):
            lanes = slice(half * HALF, (half + 1) * HALF)
            span = slice(half * 256, (half + 1) * 256)
            bent = jnp.tanh(mm(projected[:, lanes], slice_bd[...]) * 0.1)
            cool = mm(inverse_high, spread_heads[half]) + mm(inverse_low, spread_heads[half])
            scaled = (10.0 * bent) * cool
            powers = jnp.exp(scaled)
            sums = pick2(powers, same_head[...])
            over = pl.reciprocal(sums, approx=True)
            over = over * (2.0 - sums * over)
            probs = powers * (live * over)
            weights = probs.astype(BF16)
            weight_ref[part, span] = weights
            prob_ref[part, span] = probs
            slope_ref[part, span] = (1.0 - bent * bent) * cool
            scaled_ref[part, span] = scaled
            pair = jnp.concatenate([d_hidden[:, lanes], features[:, lanes]], axis=1)
            pair_ref[part, span] = pair
            right = jnp.concatenate([pair, jnp.ones((CHUNK, 128), BF16)], axis=1)
            acc_tokens[half] += mm_tn(weights, right)
        return carry

    lax.fori_loop(0, chunks, forward, 0)

    payload = token_sum.source()
    lane = lax.broadcasted_iota(jnp.int32, (SLICES, 128), 1)
    totals = jnp.zeros((SLICES, 128), F32)
    for half in range(2):
        lanes = slice(half * HALF, (half + 1) * HALF)
        dmix = jnp.where(half_diag, acc_tokens[half, :, 0:HALF], 0.0)
        numer = jnp.where(half_diag, acc_tokens[half, :, HALF : 2 * HALF], 0.0)
        payload[0:SLICES, lanes] = sum(numer[i * 64 : i * 64 + 64] for i in range(4))
        payload[SLICES : 2 * SLICES, lanes] = sum(dmix[i * 64 : i * 64 + 64] for i in range(4))
        for i in range(4):
            block = acc_tokens[half, i * 64 : i * 64 + 64, 2 * HALF : 2 * HALF + 128]
            totals = totals + jnp.where(lane == half * 4 + i, block, 0.0)
    payload[0:SLICES, WIDTH : WIDTH + 128] = totals
    payload[SLICES : 2 * SLICES, WIDTH : WIDTH + 128] = jnp.zeros((SLICES, 128), F32)

    pl.semaphore_wait(barrier, greeted)
    diag_square = block_mask((WIDTH, WIDTH), HEAD, HEAD)

    def prepare_maps():
        for k in range(3):
            square = mm(mm_tn(repeat32, wqkv_ref[k]).astype(BF16), repeat32)
            square = jnp.concatenate([square, square], axis=0)
            square = jnp.concatenate([square, square], axis=1)
            maps_ref[k] = jnp.where(diag_square, square, 0.0).astype(BF16)
        slice_t[...] = slice_bd[...].T
        wx_t[...] = wx_ref[...].T
        wfx_t[...] = wfx_ref[...].T

    def turn(source, target):
        for index in range(chunks):
            part = slice(index * CHUNK, (index + 1) * CHUNK)
            target[:, part] = source[part, :].T

    fillers = [
        prepare_maps,
        functools.partial(turn, cells_ref, cells_t),
        functools.partial(turn, cot_ref, cot_t),
        functools.partial(turn, proj_ref, proj_t),
    ]
    for index in range(len(token_stages)):
        token_sum.send(index)
        if fillers:
            fillers.pop(0)()
        token_sum.fold(index)
    for index in reversed(range(len(token_stages))):
        token_sum.gather(index)
        if fillers:
            fillers.pop(0)()
        token_sum.settle(index)
    for filler in fillers:
        filler()

    total = token_sum.total()
    numerators = total[0:SLICES, 0:WIDTH]
    d_mixed = total[SLICES : 2 * SLICES, 0:WIDTH]
    spread32 = block_mask((128, WIDTH), 1, HEAD).astype(BF16)
    denominators = pick3(total[0:SLICES, WIDTH : WIDTH + 128], spread32) + 1e-05
    tokens = numerators / denominators
    queries, key_rows, value_rows = [pick2(tokens, maps_ref[k]) for k in range(3)]

    def expand(value):
        return jnp.where(half_diag, jnp.concatenate([value] * 4, axis=0), 0.0)

    def contract(value):
        value = jnp.where(half_diag, value, 0.0)
        return sum(value[i * SLICES : (i + 1) * SLICES] for i in range(4))

    root = 1.0 / math.sqrt(HEAD)
    halves = [slice(half * HALF, (half + 1) * HALF) for half in range(2)]
    keys_bd = [expand(key_rows[:, lanes]) for lanes in halves]
    values_bd = [expand(value_rows[:, lanes]) for lanes in halves]
    d_attention = [wide(d_mixed[:, halves[i]], values_bd[i], mm_nt) for i in range(2)]
    bent = [
        jnp.tanh(wide(queries[:, halves[i]], keys_bd[i], mm_nt) * root / 10.0) for i in range(2)
    ]
    powers = [jnp.exp(10.0 * value) for value in bent]
    attention = [value / pick2(value, same_head[...]) for value in powers]
    for i in range(2):
        mixed = wide(attention[i], values_bd[i], mm)
        both_bd[i, :, 0:HALF] = expand(mixed).astype(BF16)
    shared = [attention[i] * d_attention[i] for i in range(2)]
    shared = [shared[i] - attention[i] * pick2(shared[i], same_head[...]) for i in range(2)]
    d_scores = [shared[i] * (1.0 - bent[i] * bent[i]) * root for i in range(2)]
    d_queries = jnp.concatenate([wide(d_scores[i], keys_bd[i], mm) for i in range(2)], axis=1)
    d_keys = jnp.concatenate(
        [contract(wide(d_scores[i], queries[:, halves[i]], mm_tn)) for i in range(2)], axis=1
    )
    d_values = jnp.concatenate(
        [contract(wide(attention[i], d_mixed[:, halves[i]], mm_tn)) for i in range(2)], axis=1
    )
    d_maps = (d_queries, d_keys, d_values)

    def pick_back(value, weight):
        high, low = split(value)
        return mm_nt(high, weight) + mm_nt(low, weight)

    d_tokens = sum(pick_back(d_maps[k], maps_ref[k]) for k in range(3))
    d_numer = d_tokens / denominators
    away = d_numer * tokens
    d_denom = []
    for i in range(2):
        both_bd[i, :, HALF : 2 * HALF] = expand(d_numer[:, halves[i]]).astype(BF16)
        high, low = split(expand(away[:, halves[i]]))
        ones = jnp.ones((128, HALF), BF16)
        d_denom.append(-(mm_nt(ones, high) + mm_nt(ones, low))[0:1, :])

    for half in range(2):
        both_t[half] = both_bd[half].T

    def early(index, carry):
        part = cut(index)
        for half in range(2):
            lanes = slice(half * HALF, (half + 1) * HALF)
            made = mm(weight_ref[part, half * 256 : (half + 1) * 256], both_bd[half]).astype(BF16)
            hidden_ref[part, lanes] = made[:, 0:HALF]
            dfeat_ref[part, lanes] = made[:, HALF : 2 * HALF]
        return carry

    lax.fori_loop(0, chunks, early, 0)
    source = early_sum.source()
    source[:, 0:WIDTH] = mm(cot_t[...], hidden_ref[...]).astype(BF16)
    source[:, WIDTH : 2 * WIDTH] = mm(cells_t[...], dfeat_ref[...]).astype(BF16)

    def backward(half, index, carry):
        part = cut(index)
        lanes = slice(half * HALF, (half + 1) * HALF)
        span = slice(half * 256, (half + 1) * 256)
        d_weights = mm(pair_ref[part, span], both_t[half]) + d_denom[half]
        probs = prob_ref[part, span]
        shared = probs * d_weights
        shared = shared - probs * pick2(shared, same_head[...])
        d_logits = (shared * slope_ref[part, span]).astype(BF16)
        d_temper = -pick2(shared * scaled_ref[part, span], gather_heads[half])
        d_temp = (d_temper * inverse_ref[part, :] * sigmoid_ref[part, :]).astype(BF16)
        dlogit_ref[part, :] = d_logits
        dtemp_ref[part, :] = d_temp
        dproj_ref[part, lanes] = (
            mm(d_logits, slice_t[...]) + mm(d_temp, temp_row[:, lanes])
        ).astype(BF16)
        return carry

    def fill(half, target):
        lanes = slice(half * HALF, (half + 1) * HALF)
        block = mm(proj_t[lanes, :], dlogit_ref[...])
        block = jnp.where(block_mask((HALF, 256), HEAD, SLICES), block, 0.0)
        block = block[:, 0:128] + block[:, 128:256]
        block = block + pltpu.roll(block, 64, 1)
        here = lax.broadcasted_iota(jnp.int32, (HALF, 128), 1)
        heads = lax.broadcasted_iota(jnp.int32, (HALF, 128), 0) // HEAD + 4 * half
        own = jnp.where(here == heads, mm(proj_t[lanes, :], dtemp_ref[...]), 0.0)
        own = jnp.sum(own, axis=1, keepdims=True)
        target[:, 0:128] = mm(cells_t[...], dproj_ref[:, lanes]).astype(BF16)
        target[0:HALF, 128:256] = jnp.where(here < SLICES, block, own).astype(BF16)
        target[HALF:WIDTH, 128:256] = jnp.zeros((WIDTH - HALF, 128), BF16)

    def results(index, carry):
        part = cut(index)
        result_ref[part, :] = mm(hidden_ref[part, :], wout_ref[...]).astype(BF16)
        return carry

    def cell_grads(index, carry):
        part = cut(index)
        gcells_ref[part, :] = (
            mm(dproj_ref[part, :], wx_t[...]) + mm(dfeat_ref[part, :], wfx_t[...])
        ).astype(BF16)
        return carry

    def steps(reduction):
        for index in range(len(grad_stages)):
            reduction.send(index)
            yield
            reduction.fold(index)
        for index in reversed(range(len(grad_stages))):
            reduction.gather(index)
            yield
            reduction.settle(index)

    early_steps, late_steps, last_steps = steps(early_sum), steps(late_sum), steps(last_sum)
    next(early_steps)
    lax.fori_loop(0, middle, functools.partial(backward, 0), 0)
    next(early_steps)
    lax.fori_loop(middle, chunks, functools.partial(backward, 0), 0)
    fill(0, late_sum.source())
    next(late_steps)
    next(early_steps)
    lax.fori_loop(0, middle, functools.partial(backward, 1), 0)
    next(late_steps)
    next(early_steps)
    lax.fori_loop(middle, chunks, functools.partial(backward, 1), 0)
    fill(1, last_sum.source())
    next(last_steps)
    next(late_steps)
    lax.fori_loop(0, chunks, cell_grads, 0)
    put(gcells_ref, gcells_hbm)
    next(last_steps)
    for _ in early_steps:
        pass
    lax.fori_loop(0, chunks, results, 0)
    put(result_ref, result_hbm)
    gwfx_ref[...] = early_sum.total()[:, WIDTH : 2 * WIDTH].astype(F32) * scale
    put(gwfx_ref, gwfx_hbm)
    gout_ref[...] = early_sum.total()[:, 0:WIDTH].astype(F32).T * scale
    put(gout_ref, gout_hbm)
    next(late_steps)
    for k in range(3):
        square = jnp.where(diag_square, wide(tokens, d_maps[k], mm_tn), 0.0)
        strip = sum(square[i * HEAD : (i + 1) * HEAD] for i in range(HEADS))
        strip = strip[:, 0:HALF] + strip[:, HALF:WIDTH]
        gqkv_ref[k] = pick2(strip, repeat32.T) * scale
    put(gqkv_ref, gqkv_hbm)
    next(last_steps)
    for _ in late_steps:
        pass
    gwx_ref[:, 0:HALF] = late_sum.total()[:, 0:HALF].astype(F32) * scale
    for _ in last_steps:
        pass
    gwx_ref[:, HALF:WIDTH] = last_sum.total()[:, 0:HALF].astype(F32) * scale
    put(gwx_ref, gwx_hbm)
    extra = sum(
        reduction.total()[0:HALF, 128:256].astype(F32) for reduction in (late_sum, last_sum)
    )
    extra = sum(extra[i * HEAD : (i + 1) * HEAD] for i in range(4)) * scale
    gslice_ref[...] = extra[:, 0:SLICES]
    put(gslice_ref, gslice_hbm)
    unit = (
        lax.broadcasted_iota(jnp.int32, (HEAD, HEAD), 0)
        == lax.broadcasted_iota(jnp.int32, (HEAD, HEAD), 1)
    ).astype(BF16)
    gtemp_ref[...] = pick3(extra, unit, mm_tn)[SLICES : SLICES + 1, :]
    put(gtemp_ref, gtemp_hbm)
    for copy in outgoing:
        copy.wait()


def hand_over(*refs):
    count = (len(refs) - 2) // 3
    sources, targets, between = refs[:count], refs[count : 2 * count], refs[2 * count : 3 * count]
    arrive, leave = refs[-2:]
    copies = [pltpu.make_async_copy(sources[i], between[i], arrive.at[i]) for i in range(count)]
    for copy in copies:
        copy.start()
    onward = []
    for i, copy in enumerate(copies):
        copy.wait()
        onward.append(pltpu.make_async_copy(between[i], targets[i], leave.at[i]))
        onward[-1].start()
    for copy in onward:
        copy.wait()


def body(devices, cells, counts, w_x, w_fx, w_slice, w_temp, w_qkv, w_out, cotangent):
    rows = cells.shape[0]
    token_stages = stages_of(devices, 2 * SLICES, 8)
    grad_stages = stages_of(devices, WIDTH, 16)
    scale = 1.0 / math.sqrt(rows * devices)
    anywhere = pl.BlockSpec(memory_space=pl.ANY)
    vmem = pltpu.VMEM
    out_shapes = [
        ((rows, WIDTH), BF16),
        ((rows, WIDTH), BF16),
        ((WIDTH, WIDTH), F32),
        ((WIDTH, WIDTH), F32),
        ((HEAD, SLICES), F32),
        ((1, HEAD), F32),
        ((3, HEAD, HEAD), F32),
        ((WIDTH, WIDTH), F32),
    ]
    out_shape = tuple(jax.ShapeDtypeStruct(*one) for one in out_shapes)
    outs = pl.pallas_call(
        functools.partial(layer_kernel, token_stages, grad_stages, scale),
        out_shape=out_shape,
        in_specs=[anywhere] * 9,
        out_specs=[anywhere] * 8,
        scratch_shapes=[
            pltpu.SMEM((1,), jnp.int32),
            vmem((rows, WIDTH), BF16),
            vmem((rows, WIDTH), BF16),
            vmem((WIDTH, WIDTH), BF16),
            vmem((WIDTH, WIDTH), BF16),
            vmem((HEAD, SLICES), BF16),
            vmem((1, HEAD), BF16),
            vmem((3, HEAD, HEAD), BF16),
            vmem((WIDTH, WIDTH), BF16),
        ]
        + [vmem(*one) for one in out_shapes]
        + [
            pltpu.SemaphoreType.DMA((9,)),
            pltpu.SemaphoreType.DMA((8,)),
            vmem((rows, WIDTH), BF16),
            vmem((rows, SPREAD), BF16),
            vmem((rows, SPREAD), BF16),
            vmem((rows, SPREAD), F32),
            vmem((rows, SPREAD), F32),
            vmem((rows, SPREAD), F32),
            vmem((rows, 128), F32),
            vmem((rows, 128), F32),
            vmem((WIDTH, rows), BF16),
            vmem((WIDTH, rows), BF16),
            vmem((WIDTH, rows), BF16),
            vmem((rows, WIDTH), BF16),
            vmem((rows, WIDTH), BF16),
            vmem((rows, WIDTH), BF16),
            vmem((rows, 256), BF16),
            vmem((rows, 128), BF16),
            vmem((HALF, 256), BF16),
            vmem((WIDTH, 128), BF16),
            vmem((128, WIDTH), BF16),
            vmem((256, 256), BF16),
            vmem((3, WIDTH, WIDTH), BF16),
            vmem((2, 256, 2 * HALF + 128), F32),
            vmem((2, 256, 2 * HALF), BF16),
            vmem((2, 256, 2 * HALF), BF16),
            vmem((256, HALF), BF16),
            vmem((WIDTH, WIDTH), BF16),
            vmem((WIDTH, WIDTH), BF16),
            vmem((WIDTH, WIDTH), BF16),
        ]
        + Reduction.scratch(token_stages, WIDTH + 128, F32)
        + Reduction.scratch(grad_stages, 2 * WIDTH, BF16)
        + Reduction.scratch(grad_stages, 256, BF16)
        + Reduction.scratch(grad_stages, 256, BF16),
        compiler_params=pltpu.CompilerParams(
            collective_id=0, has_side_effects=True, vmem_limit_bytes=60 * 1024 * 1024
        ),
    )(counts, cells, cotangent, w_x, w_fx, w_slice, w_temp.reshape(1, HEAD), w_qkv, w_out)
    outs = pl.pallas_call(
        hand_over,
        out_shape=out_shape,
        in_specs=[anywhere] * 8,
        out_specs=[anywhere] * 8,
        scratch_shapes=[vmem(*one) for one in out_shapes] + [pltpu.SemaphoreType.DMA((8,))] * 2,
        compiler_params=pltpu.CompilerParams(vmem_limit_bytes=60 * 1024 * 1024),
    )(*outs)
    result, gcells, gwx, gwfx, gslice, gtemp, gqkv, gout = outs
    return result, gcells, gwx, gwfx, gslice, gtemp.reshape(HEAD), gqkv, gout


def solution(mesh):
    placed = (
        P(("groups", "dom"), None),
        P(("groups", "dom")),
        P(),
        P(),
        P(),
        P(),
        P(),
        P(),
        P(("groups", "dom"), None),
    )
    return jax.shard_map(
        functools.partial(body, mesh.shape["dom"]),
        mesh=mesh,
        in_specs=placed,
        out_specs=(
            P(("groups", "dom"), None),
            P(("groups", "dom"), None),
            P("groups", None),
            P("groups", None),
            P("groups", None),
            P("groups"),
            P("groups", None, None),
            P("groups", None),
        ),
        check_vma=False,
    )
```

```python
import functools
import math

import jax
import jax.numpy as jnp
from jax import lax
from jax.experimental import pallas as pl
from jax.experimental.pallas import tpu as pltpu
from jax.sharding import PartitionSpec as P

HEAD = 32
SLICES = 64
HEADS = 8
WIDTH = HEAD * HEADS
SPREAD = SLICES * HEADS
HALF = WIDTH // 2
CHUNK = 256
F32 = jnp.float32
BF16 = jnp.bfloat16
MESH = pl.DeviceIdType.MESH


def mm(left, right):
    return jnp.dot(left, right, preferred_element_type=F32)


def mm_nt(left, right):
    return lax.dot_general(left, right, (((1,), (1,)), ((), ())), preferred_element_type=F32)


def mm_tn(left, right):
    return lax.dot_general(left, right, (((0,), (0,)), ((), ())), preferred_element_type=F32)


def split(value):
    high = value.astype(BF16)
    return high, (value - high.astype(F32)).astype(BF16)


def pick2(value, ones):
    high, low = split(value)
    return mm(high, ones) + mm(low, ones)


def pick3(value, ones, product=mm):
    high = value.astype(BF16)
    rest = value - high.astype(F32)
    middle, low = split(rest)
    return product(high, ones) + product(middle, ones) + product(low, ones)


def wide(left, right, product):
    left_high, left_low = split(left)
    right_high, right_low = split(right)
    return (
        product(left_high, right_high)
        + product(left_high, right_low)
        + product(left_low, right_high)
    )


def block_mask(shape, row_width, column_width):
    rows = lax.broadcasted_iota(jnp.int32, shape, 0)
    columns = lax.broadcasted_iota(jnp.int32, shape, 1)
    return (rows // row_width) == (columns // column_width)


def stages_of(devices, rows, tile):
    sizes, rest = [2], devices // 2
    while rest > 1:
        size = min(8, rest)
        sizes.append(size)
        rest //= size
    stages, stride = [], 1
    for size in sizes:
        scattered = rows % (size * tile) == 0
        stages.append((size, stride, rows, scattered))
        rows = rows // size if scattered else rows
        stride *= size
    return stages


def peers_of(stage):
    size, stride, _, _ = stage
    me = lax.axis_index("dom")
    place = lax.rem(lax.div(me, stride), size)
    others = []
    for step in range(1, size):
        there = lax.rem(place + step, size)
        others.append((there, me + (there - place) * stride))
    return place, others


class Reduction:
    @staticmethod
    def scratch(stages, columns, dtype):
        shapes = []
        for size, _, rows, scattered in stages:
            part = rows // size if scattered else rows
            shapes += [
                pltpu.VMEM((rows, columns), dtype),
                pltpu.VMEM((size, part, columns), dtype),
                pltpu.VMEM((rows, columns), dtype),
                pltpu.SemaphoreType.DMA((4, size)),
            ]
        return shapes

    def __init__(self, stages, refs):
        self.stages = stages
        self.levels = [refs[4 * i : 4 * i + 4] for i in range(len(stages))]

    def source(self):
        return self.levels[0][0]

    def total(self):
        return self.levels[0][2]

    def send(self, index):
        stage = self.stages[index]
        size, _, rows, scattered = stage
        source, received, _, sems = self.levels[index]
        place, others = peers_of(stage)
        part = rows // size if scattered else rows
        self.flying = []
        for step, (there, device) in enumerate(others):
            cut = source
            if scattered:
                cut = source.at[pl.ds(pl.multiple_of(there * part, part), part), :]
            copy = pltpu.make_async_remote_copy(
                src_ref=cut,
                dst_ref=received.at[place],
                send_sem=sems.at[0, step],
                recv_sem=sems.at[1, step],
                device_id={"dom": device},
                device_id_type=MESH,
            )
            copy.start()
            self.flying.append(copy)
        if scattered:
            received[place] = source[pl.ds(pl.multiple_of(place * part, part), part), :]
        else:
            received[place] = source[...]

    def fold(self, index):
        size, _, rows, scattered = self.stages[index]
        source, received, gathered, _ = self.levels[index]
        for copy in self.flying:
            copy.wait()
        total = received[0].astype(F32)
        for slot in range(1, size):
            total = total + received[slot].astype(F32)
        total = total.astype(source.dtype)
        if index + 1 < len(self.stages):
            self.levels[index + 1][0][...] = total
        else:
            self.place(index, total)

    def place(self, index, value):
        size, _, rows, scattered = self.stages[index]
        gathered = self.levels[index][2]
        if scattered:
            part = rows // size
            place, _ = peers_of(self.stages[index])
            gathered[pl.ds(pl.multiple_of(place * part, part), part), :] = value
        else:
            gathered[...] = value

    def gather(self, index):
        stage = self.stages[index]
        size, _, rows, scattered = stage
        gathered, sems = self.levels[index][2:]
        self.flying = []
        if not scattered:
            return
        part = rows // size
        place, others = peers_of(stage)
        mine = gathered.at[pl.ds(pl.multiple_of(place * part, part), part), :]
        for step, (_, device) in enumerate(others):
            copy = pltpu.make_async_remote_copy(
                src_ref=mine,
                dst_ref=mine,
                send_sem=sems.at[2, step],
                recv_sem=sems.at[3, step],
                device_id={"dom": device},
                device_id_type=MESH,
            )
            copy.start()
            self.flying.append(copy)

    def settle(self, index):
        for copy in self.flying:
            copy.wait()
        if index > 0:
            self.place(index - 1, self.levels[index][2][...])

    def last(self):
        return len(self.stages) - 1


def layer_kernel(
    token_stages,
    grad_stages,
    scale,
    counts_hbm,
    cells_hbm,
    cot_hbm,
    wx_hbm,
    wfx_hbm,
    wslice_hbm,
    wtemp_hbm,
    wqkv_hbm,
    wout_hbm,
    result_hbm,
    gcells_hbm,
    gwx_hbm,
    gwfx_hbm,
    gslice_hbm,
    gtemp_hbm,
    gqkv_hbm,
    gout_hbm,
    counts_ref,
    cells_ref,
    cot_ref,
    wx_ref,
    wfx_ref,
    wslice_ref,
    wtemp_ref,
    wqkv_ref,
    wout_ref,
    result_ref,
    gcells_ref,
    gwx_ref,
    gwfx_ref,
    gslice_ref,
    gtemp_ref,
    gqkv_ref,
    gout_ref,
    in_sems,
    out_sems,
    proj_ref,
    pair_ref,
    weight_ref,
    prob_ref,
    slope_ref,
    scaled_ref,
    inverse_ref,
    sigmoid_ref,
    cells_t,
    cot_t,
    proj_t,
    hidden_ref,
    dfeat_ref,
    dproj_ref,
    dlogit_ref,
    dtemp_ref,
    slice_bd,
    temp_bd,
    temp_row,
    same_head,
    maps_ref,
    acc_tokens,
    both_bd,
    both_t,
    slice_t,
    wout_t,
    wx_t,
    wfx_t,
    *sum_refs,
):
    rows = cells_ref.shape[0]
    chunks = rows // CHUNK
    middle = chunks // 2
    levels = 4 * len(token_stages)
    levels_g = 4 * len(grad_stages)
    token_sums = [
        Reduction(token_stages, sum_refs[i * levels : (i + 1) * levels]) for i in range(2)
    ]
    sum_refs = sum_refs[2 * levels :]
    early_sum, late_sum, last_sum = [
        Reduction(grad_stages, sum_refs[i * levels_g : (i + 1) * levels_g]) for i in range(3)
    ]

    pairs = (
        (wslice_hbm, wslice_ref),
        (wtemp_hbm, wtemp_ref),
        (cells_hbm, cells_ref),
        (wx_hbm, wx_ref),
        (counts_hbm, counts_ref),
        (wfx_hbm, wfx_ref),
        (wout_hbm, wout_ref),
        (cot_hbm, cot_ref),
        (wqkv_hbm, wqkv_ref),
    )
    incoming = [
        pltpu.make_async_copy(there, here, in_sems.at[i]) for i, (there, here) in enumerate(pairs)
    ]
    for copy in incoming:
        copy.start()
    barrier = pltpu.get_barrier_semaphore()
    greeted = 0
    for stage in token_stages:
        for _, device in peers_of(stage)[1]:
            pl.semaphore_signal(barrier, inc=1, device_id={"dom": device}, device_id_type=MESH)
            greeted += 1
    outgoing = []

    def put(source, target):
        copy = pltpu.make_async_copy(source, target, out_sems.at[len(outgoing)])
        copy.start()
        outgoing.append(copy)

    repeat32 = (
        (lax.broadcasted_iota(jnp.int32, (HEAD, HALF), 1) % HEAD)
        == lax.broadcasted_iota(jnp.int32, (HEAD, HALF), 0)
    ).astype(BF16)
    repeat64 = (
        (lax.broadcasted_iota(jnp.int32, (SLICES, 256), 1) % SLICES)
        == lax.broadcasted_iota(jnp.int32, (SLICES, 256), 0)
    ).astype(BF16)
    lane_head = lax.broadcasted_iota(jnp.int32, (256, 128), 1)
    row_head = lax.broadcasted_iota(jnp.int32, (256, 128), 0) // SLICES
    gather_heads = [(row_head + 4 * half == lane_head).astype(BF16) for half in range(2)]
    spread_lane = lax.broadcasted_iota(jnp.int32, (128, 256), 1) // SLICES
    spread_row = lax.broadcasted_iota(jnp.int32, (128, 256), 0)
    spread_heads = [(spread_lane + 4 * half == spread_row).astype(BF16) for half in range(2)]
    half_diag = block_mask((256, HALF), SLICES, HEAD)
    same_head[...] = block_mask((256, 256), SLICES, SLICES).astype(BF16)

    incoming[0].wait()
    incoming[1].wait()
    tall = mm_tn(repeat32, wslice_ref[...]).astype(BF16)
    slice_bd[...] = jnp.where(
        block_mask((HALF, 256), HEAD, SLICES), mm(tall, repeat64), 0.0
    ).astype(BF16)
    temp_rows = jnp.broadcast_to(wtemp_ref[...], (128, HEAD))
    column = mm_nt(repeat32.T, temp_rows)
    line = mm(temp_rows, repeat32)
    for half in range(2):
        place = slice(half * HALF, (half + 1) * HALF)
        lanes = lax.broadcasted_iota(jnp.int32, (HALF, 128), 1)
        heads = lax.broadcasted_iota(jnp.int32, (HALF, 128), 0) // HEAD + 4 * half
        temp_bd[place, :] = jnp.where(lanes == heads, column, 0.0).astype(BF16)
        heads = lax.broadcasted_iota(jnp.int32, (128, HALF), 1) // HEAD + 4 * half
        here = lax.broadcasted_iota(jnp.int32, (128, HALF), 0)
        temp_row[:, place] = jnp.where(here == heads, line, 0.0).astype(BF16)
    acc_tokens[...] = jnp.zeros_like(acc_tokens)
    for copy in incoming[2:]:
        copy.wait()
    wout_t[...] = wout_ref[...].T
    count = counts_ref[0]

    def cut(index):
        return pl.ds(pl.multiple_of(index * CHUNK, CHUNK), CHUNK)

    def project(index, carry):
        part = cut(index)
        cells = cells_ref[part, :]
        projected = mm(cells, wx_ref[...]).astype(BF16)
        features = mm(cells, wfx_ref[...]).astype(BF16)
        d_hidden = mm(cot_ref[part, :], wout_t[...]).astype(BF16)
        temp_lin = mm(projected, temp_bd[...])
        away = jnp.exp(-jnp.abs(temp_lin))
        temper = 0.5 + (jnp.maximum(temp_lin, 0.0) + jnp.log(1.0 + away))
        proj_ref[part, :] = projected
        inverse_ref[part, :] = 1.0 / temper
        sigmoid_ref[part, :] = jnp.where(temp_lin >= 0.0, 1.0, away) / (1.0 + away)
        for half in range(2):
            lanes = slice(half * HALF, (half + 1) * HALF)
            pair_ref[part, half * 256 : half * 256 + HALF] = d_hidden[:, lanes]
            pair_ref[part, half * 256 + HALF : half * 256 + 256] = features[:, lanes]
        return carry

    def forward(half, index, carry):
        part = cut(index)
        lanes = slice(half * HALF, (half + 1) * HALF)
        span = slice(half * 256, (half + 1) * 256)
        place = lax.broadcasted_iota(jnp.int32, (CHUNK, 1), 0) + index * CHUNK
        live = (place < count).astype(F32)
        bent = jnp.tanh(mm(proj_ref[part, lanes], slice_bd[...]) * 0.1)
        cool = pick2(inverse_ref[part, :], spread_heads[half])
        scaled = (10.0 * bent) * cool
        powers = jnp.exp(scaled)
        sums = pick2(powers, same_head[...])
        over = pl.reciprocal(sums, approx=True)
        over = over * (2.0 - sums * over)
        probs = powers * (live * over)
        weights = probs.astype(BF16)
        weight_ref[part, span] = weights
        prob_ref[part, span] = probs
        slope_ref[part, span] = (1.0 - bent * bent) * cool
        scaled_ref[part, span] = scaled
        right = jnp.concatenate([pair_ref[part, span], jnp.ones((CHUNK, 128), BF16)], axis=1)
        acc_tokens[half] += mm_tn(weights, right)
        return carry

    lane = lax.broadcasted_iota(jnp.int32, (SLICES, 128), 1)

    def pay(half):
        payload = token_sums[half].source()
        dmix = jnp.where(half_diag, acc_tokens[half, :, 0:HALF], 0.0)
        numer = jnp.where(half_diag, acc_tokens[half, :, HALF : 2 * HALF], 0.0)
        payload[0:SLICES, 0:HALF] = sum(numer[i * 64 : i * 64 + 64] for i in range(4))
        payload[SLICES : 2 * SLICES, 0:HALF] = sum(dmix[i * 64 : i * 64 + 64] for i in range(4))
        totals = jnp.zeros((SLICES, 128), F32)
        for i in range(4):
            block = acc_tokens[half, i * 64 : i * 64 + 64, 2 * HALF : 2 * HALF + 128]
            totals = totals + jnp.where(lane == i, block, 0.0)
        payload[0:SLICES, HALF : HALF + 128] = totals
        payload[SLICES : 2 * SLICES, HALF : HALF + 128] = jnp.zeros((SLICES, 128), F32)

    diag_square = block_mask((HALF, HALF), HEAD, HEAD)

    def prepare_maps():
        for k in range(3):
            square = mm(mm_tn(repeat32, wqkv_ref[k]).astype(BF16), repeat32)
            maps_ref[k] = jnp.where(diag_square, square, 0.0).astype(BF16)
        slice_t[...] = slice_bd[...].T
        wx_t[...] = wx_ref[...].T
        wfx_t[...] = wfx_ref[...].T

    def turn(source, target):
        for index in range(chunks):
            part = slice(index * CHUNK, (index + 1) * CHUNK)
            target[:, part] = source[part, :].T

    def steps(reduction):
        count_of_stages = len(reduction.stages)
        for index in range(count_of_stages):
            reduction.send(index)
            yield
            reduction.fold(index)
        for index in reversed(range(count_of_stages)):
            reduction.gather(index)
            yield
            reduction.settle(index)

    def finish(moves):
        for _ in moves:
            pass

    def expand(value):
        return jnp.where(half_diag, jnp.concatenate([value] * 4, axis=0), 0.0)

    def contract(value):
        value = jnp.where(half_diag, value, 0.0)
        return sum(value[i * SLICES : (i + 1) * SLICES] for i in range(4))

    def pick_back(value, weight):
        high, low = split(value)
        return mm_nt(high, weight) + mm_nt(low, weight)

    root = 1.0 / math.sqrt(HEAD)

    def attend(half):
        total = token_sums[half].total()
        numerators = total[0:SLICES, 0:HALF]
        d_mixed = total[SLICES : 2 * SLICES, 0:HALF]
        spread32 = block_mask((128, HALF), 1, HEAD).astype(BF16)
        denominators = pick3(total[0:SLICES, HALF : HALF + 128], spread32) + 1e-05
        tokens = numerators / denominators
        queries, key_rows, value_rows = [pick2(tokens, maps_ref[k]) for k in range(3)]
        keys_bd = expand(key_rows)
        values_bd = expand(value_rows)
        d_attention = wide(d_mixed, values_bd, mm_nt)
        bent = jnp.tanh(wide(queries, keys_bd, mm_nt) * (root / 10.0))
        powers = jnp.exp(10.0 * bent)
        attention = powers / pick2(powers, same_head[...])
        mixed_half = expand(wide(attention, values_bd, mm)).astype(BF16)
        shared = attention * d_attention
        shared = shared - attention * pick2(shared, same_head[...])
        d_scores = shared * (1.0 - bent * bent) * root
        d_queries = wide(d_scores, keys_bd, mm)
        d_keys = contract(wide(d_scores, queries, mm_tn))
        d_values = contract(wide(attention, d_mixed, mm_tn))
        d_maps = (d_queries, d_keys, d_values)
        d_tokens = sum(pick_back(d_maps[k], maps_ref[k]) for k in range(3))
        d_numer = d_tokens / denominators
        dnumer_half = expand(d_numer).astype(BF16)
        both = jnp.concatenate([mixed_half, dnumer_half], axis=1)
        both_bd[half] = both
        both_t[half] = both.T
        high, low = split(expand(d_numer * tokens))
        ones = jnp.ones((128, HALF), BF16)
        d_denom = -(mm_nt(ones, high) + mm_nt(ones, low))[0:1, :]
        return tokens, d_maps, d_denom

    def early(half, index, carry):
        part = cut(index)
        lanes = slice(half * HALF, (half + 1) * HALF)
        made = mm(weight_ref[part, half * 256 : (half + 1) * 256], both_bd[half]).astype(BF16)
        hidden_ref[part, lanes] = made[:, 0:HALF]
        dfeat_ref[part, lanes] = made[:, HALF : 2 * HALF]
        return carry

    def fill_early(half, target):
        lanes = slice(half * HALF, (half + 1) * HALF)
        target[:, 0:128] = mm(cot_t[...], hidden_ref[:, lanes]).astype(BF16)
        target[:, 128:256] = mm(cells_t[...], dfeat_ref[:, lanes]).astype(BF16)

    def backward(half, d_denom, index, carry):
        part = cut(index)
        lanes = slice(half * HALF, (half + 1) * HALF)
        span = slice(half * 256, (half + 1) * 256)
        d_weights = mm(pair_ref[part, span], both_t[half]) + d_denom
        probs = prob_ref[part, span]
        shared = probs * d_weights
        shared = shared - probs * pick2(shared, same_head[...])
        d_logits = (shared * slope_ref[part, span]).astype(BF16)
        d_temper = -pick2(shared * scaled_ref[part, span], gather_heads[half])
        d_temp = (d_temper * inverse_ref[part, :] * sigmoid_ref[part, :]).astype(BF16)
        dlogit_ref[part, :] = d_logits
        dtemp_ref[part, :] = d_temp
        dproj_ref[part, lanes] = (
            mm(d_logits, slice_t[...]) + mm(d_temp, temp_row[:, lanes])
        ).astype(BF16)
        return carry

    def fill_late(half, target, start):
        lanes = slice(half * HALF, (half + 1) * HALF)
        block = mm(proj_t[lanes, :], dlogit_ref[...])
        block = jnp.where(block_mask((HALF, 256), HEAD, SLICES), block, 0.0)
        block = block[:, 0:128] + block[:, 128:256]
        block = block + pltpu.roll(block, 64, 1)
        here = lax.broadcasted_iota(jnp.int32, (HALF, 128), 1)
        heads = lax.broadcasted_iota(jnp.int32, (HALF, 128), 0) // HEAD + 4 * half
        own = jnp.where(here == heads, mm(proj_t[lanes, :], dtemp_ref[...]), 0.0)
        own = jnp.sum(own, axis=1, keepdims=True)
        extra = slice(start + 128, start + 256)
        target[:, start : start + 128] = mm(cells_t[...], dproj_ref[:, lanes]).astype(BF16)
        target[0:HALF, extra] = jnp.where(here < SLICES, block, own).astype(BF16)
        target[HALF:WIDTH, extra] = jnp.zeros((WIDTH - HALF, 128), BF16)

    def results(index, carry):
        part = cut(index)
        result_ref[part, :] = mm(hidden_ref[part, :], wout_ref[...]).astype(BF16)
        return carry

    def cell_grads(index, carry):
        part = cut(index)
        gcells_ref[part, :] = (
            mm(dproj_ref[part, :], wx_t[...]) + mm(dfeat_ref[part, :], wfx_t[...])
        ).astype(BF16)
        return carry

    def loop(step, first=0, end=chunks):
        lax.fori_loop(first, end, step, 0)

    bind = functools.partial
    loop(project)
    loop(bind(forward, 0))
    pay(0)
    pl.semaphore_wait(barrier, greeted)
    first_moves, second_moves = [steps(reduction) for reduction in token_sums]
    next(first_moves)
    loop(bind(forward, 1), 0, middle)
    next(first_moves)
    loop(bind(forward, 1), middle, chunks)
    pay(1)
    next(second_moves)
    next(first_moves)
    prepare_maps()
    turn(cells_ref, cells_t)
    next(second_moves)
    next(first_moves)
    turn(cot_ref, cot_t)
    turn(proj_ref, proj_t)
    finish(first_moves)

    tokens0, d_maps0, d_denom0 = attend(0)
    next(second_moves)
    loop(bind(early, 0))
    loop(bind(backward, 0, d_denom0), 0, middle)
    next(second_moves)
    loop(bind(backward, 0, d_denom0), middle, chunks)
    fill_early(0, early_sum.source())
    fill_late(0, early_sum.source(), 256)
    early_moves, late_moves, last_moves = [
        steps(reduction) for reduction in (early_sum, late_sum, last_sum)
    ]
    next(early_moves)
    finish(second_moves)

    tokens1, d_maps1, d_denom1 = attend(1)
    next(early_moves)
    loop(bind(early, 1))
    fill_early(1, late_sum.source())
    next(late_moves)
    loop(bind(backward, 1, d_denom1), 0, middle)
    next(early_moves)
    next(late_moves)
    loop(bind(backward, 1, d_denom1), middle, chunks)
    fill_late(1, last_sum.source(), 0)
    next(last_moves)
    next(early_moves)
    next(late_moves)
    loop(cell_grads)
    put(gcells_ref, gcells_hbm)
    next(last_moves)
    finish(early_moves)
    next(late_moves)
    loop(results)
    put(result_ref, result_hbm)
    for k in range(3):
        square = wide(tokens0, d_maps0[k], mm_tn) + wide(tokens1, d_maps1[k], mm_tn)
        square = jnp.where(diag_square, square, 0.0)
        strip = sum(square[i * HEAD : (i + 1) * HEAD] for i in range(4))
        gqkv_ref[k] = pick2(strip, repeat32.T) * scale
    put(gqkv_ref, gqkv_hbm)
    gwfx_ref[:, 0:HALF] = early_sum.total()[:, 128:256].astype(F32) * scale
    gout_ref[0:HALF, :] = early_sum.total()[:, 0:128].astype(F32).T * scale
    gwx_ref[:, 0:HALF] = early_sum.total()[:, 256:384].astype(F32) * scale
    next(last_moves)
    finish(late_moves)
    gwfx_ref[:, HALF:WIDTH] = late_sum.total()[:, 128:256].astype(F32) * scale
    put(gwfx_ref, gwfx_hbm)
    gout_ref[HALF:WIDTH, :] = late_sum.total()[:, 0:128].astype(F32).T * scale
    put(gout_ref, gout_hbm)
    next(last_moves)
    finish(last_moves)
    gwx_ref[:, HALF:WIDTH] = last_sum.total()[:, 0:HALF].astype(F32) * scale
    put(gwx_ref, gwx_hbm)
    extra = early_sum.total()[0:HALF, 384:512].astype(F32)
    extra = extra + last_sum.total()[0:HALF, 128:256].astype(F32)
    extra = sum(extra[i * HEAD : (i + 1) * HEAD] for i in range(4)) * scale
    gslice_ref[...] = extra[:, 0:SLICES]
    put(gslice_ref, gslice_hbm)
    unit = (
        lax.broadcasted_iota(jnp.int32, (HEAD, HEAD), 0)
        == lax.broadcasted_iota(jnp.int32, (HEAD, HEAD), 1)
    ).astype(BF16)
    gtemp_ref[...] = pick3(extra, unit, mm_tn)[SLICES : SLICES + 1, :]
    put(gtemp_ref, gtemp_hbm)
    for copy in outgoing:
        copy.wait()


def hand_over(*refs):
    count = (len(refs) - 2) // 3
    sources, targets, between = refs[:count], refs[count : 2 * count], refs[2 * count : 3 * count]
    arrive, leave = refs[-2:]
    copies = [pltpu.make_async_copy(sources[i], between[i], arrive.at[i]) for i in range(count)]
    for copy in copies:
        copy.start()
    onward = []
    for i, copy in enumerate(copies):
        copy.wait()
        onward.append(pltpu.make_async_copy(between[i], targets[i], leave.at[i]))
        onward[-1].start()
    for copy in onward:
        copy.wait()


def body(devices, cells, counts, w_x, w_fx, w_slice, w_temp, w_qkv, w_out, cotangent):
    rows = cells.shape[0]
    token_stages = stages_of(devices, 2 * SLICES, 8)
    grad_stages = stages_of(devices, WIDTH, 16)
    scale = 1.0 / math.sqrt(rows * devices)
    anywhere = pl.BlockSpec(memory_space=pl.ANY)
    vmem = pltpu.VMEM
    out_shapes = [
        ((rows, WIDTH), BF16),
        ((rows, WIDTH), BF16),
        ((WIDTH, WIDTH), F32),
        ((WIDTH, WIDTH), F32),
        ((HEAD, SLICES), F32),
        ((1, HEAD), F32),
        ((3, HEAD, HEAD), F32),
        ((WIDTH, WIDTH), F32),
    ]
    out_shape = tuple(jax.ShapeDtypeStruct(*one) for one in out_shapes)
    outs = pl.pallas_call(
        functools.partial(layer_kernel, token_stages, grad_stages, scale),
        out_shape=out_shape,
        in_specs=[anywhere] * 9,
        out_specs=[anywhere] * 8,
        scratch_shapes=[
            pltpu.SMEM((1,), jnp.int32),
            vmem((rows, WIDTH), BF16),
            vmem((rows, WIDTH), BF16),
            vmem((WIDTH, WIDTH), BF16),
            vmem((WIDTH, WIDTH), BF16),
            vmem((HEAD, SLICES), BF16),
            vmem((1, HEAD), BF16),
            vmem((3, HEAD, HEAD), BF16),
            vmem((WIDTH, WIDTH), BF16),
        ]
        + [vmem(*one) for one in out_shapes]
        + [
            pltpu.SemaphoreType.DMA((9,)),
            pltpu.SemaphoreType.DMA((8,)),
            vmem((rows, WIDTH), BF16),
            vmem((rows, SPREAD), BF16),
            vmem((rows, SPREAD), BF16),
            vmem((rows, SPREAD), F32),
            vmem((rows, SPREAD), F32),
            vmem((rows, SPREAD), F32),
            vmem((rows, 128), F32),
            vmem((rows, 128), F32),
            vmem((WIDTH, rows), BF16),
            vmem((WIDTH, rows), BF16),
            vmem((WIDTH, rows), BF16),
            vmem((rows, WIDTH), BF16),
            vmem((rows, WIDTH), BF16),
            vmem((rows, WIDTH), BF16),
            vmem((rows, 256), BF16),
            vmem((rows, 128), BF16),
            vmem((HALF, 256), BF16),
            vmem((WIDTH, 128), BF16),
            vmem((128, WIDTH), BF16),
            vmem((256, 256), BF16),
            vmem((3, HALF, HALF), BF16),
            vmem((2, 256, 2 * HALF + 128), F32),
            vmem((2, 256, 2 * HALF), BF16),
            vmem((2, 256, 2 * HALF), BF16),
            vmem((256, HALF), BF16),
            vmem((WIDTH, WIDTH), BF16),
            vmem((WIDTH, WIDTH), BF16),
            vmem((WIDTH, WIDTH), BF16),
        ]
        + Reduction.scratch(token_stages, HALF + 128, F32) * 2
        + Reduction.scratch(grad_stages, 2 * WIDTH, BF16)
        + Reduction.scratch(grad_stages, 256, BF16)
        + Reduction.scratch(grad_stages, 256, BF16),
        compiler_params=pltpu.CompilerParams(
            collective_id=0, has_side_effects=True, vmem_limit_bytes=60 * 1024 * 1024
        ),
    )(counts, cells, cotangent, w_x, w_fx, w_slice, w_temp.reshape(1, HEAD), w_qkv, w_out)
    outs = pl.pallas_call(
        hand_over,
        out_shape=out_shape,
        in_specs=[anywhere] * 8,
        out_specs=[anywhere] * 8,
        scratch_shapes=[vmem(*one) for one in out_shapes] + [pltpu.SemaphoreType.DMA((8,))] * 2,
        compiler_params=pltpu.CompilerParams(vmem_limit_bytes=60 * 1024 * 1024),
    )(*outs)
    result, gcells, gwx, gwfx, gslice, gtemp, gqkv, gout = outs
    return result, gcells, gwx, gwfx, gslice, gtemp.reshape(HEAD), gqkv, gout


def solution(mesh):
    placed = (
        P(("groups", "dom"), None),
        P(("groups", "dom")),
        P(),
        P(),
        P(),
        P(),
        P(),
        P(),
        P(("groups", "dom"), None),
    )
    return jax.shard_map(
        functools.partial(body, mesh.shape["dom"]),
        mesh=mesh,
        in_specs=placed,
        out_specs=(
            P(("groups", "dom"), None),
            P(("groups", "dom"), None),
            P("groups", None),
            P("groups", None),
            P("groups", None),
            P("groups"),
            P("groups", None, None),
            P("groups", None),
        ),
        check_vma=False,
    )
```

```python
import functools
import math

import jax
import jax.numpy as jnp
from jax import lax
from jax.experimental import pallas as pl
from jax.experimental.pallas import tpu as pltpu
from jax.sharding import PartitionSpec as P

HEAD = 32
SLICES = 64
HEADS = 8
WIDTH = HEAD * HEADS
SPREAD = SLICES * HEADS
HALF = WIDTH // 2
CHUNK = 256
F32 = jnp.float32
BF16 = jnp.bfloat16
MESH = pl.DeviceIdType.MESH


def mm(left, right):
    return jnp.dot(left, right, preferred_element_type=F32)


def mm_nt(left, right):
    return lax.dot_general(left, right, (((1,), (1,)), ((), ())), preferred_element_type=F32)


def mm_tn(left, right):
    return lax.dot_general(left, right, (((0,), (0,)), ((), ())), preferred_element_type=F32)


def split(value):
    high = value.astype(BF16)
    return high, (value - high.astype(F32)).astype(BF16)


def pick2(value, ones):
    high, low = split(value)
    return mm(high, ones) + mm(low, ones)


def pick3(value, ones, product=mm):
    high = value.astype(BF16)
    rest = value - high.astype(F32)
    middle, low = split(rest)
    return product(high, ones) + product(middle, ones) + product(low, ones)


def wide(left, right, product):
    left_high, left_low = split(left)
    right_high, right_low = split(right)
    return (
        product(left_high, right_high)
        + product(left_high, right_low)
        + product(left_low, right_high)
    )


def block_mask(shape, row_width, column_width):
    rows = lax.broadcasted_iota(jnp.int32, shape, 0)
    columns = lax.broadcasted_iota(jnp.int32, shape, 1)
    return (rows // row_width) == (columns // column_width)


def stages_of(devices, rows, tile):
    sizes, rest = [2], devices // 2
    while rest > 1:
        size = min(8, rest)
        sizes.append(size)
        rest //= size
    stages, stride = [], 1
    for size in sizes:
        scattered = rows % (size * tile) == 0
        stages.append((size, stride, rows, scattered))
        rows = rows // size if scattered else rows
        stride *= size
    return stages


def peers_of(stage):
    size, stride, _, _ = stage
    me = lax.axis_index("dom")
    place = lax.rem(lax.div(me, stride), size)
    others = []
    for step in range(1, size):
        there = lax.rem(place + step, size)
        others.append((there, me + (there - place) * stride))
    return place, others


class Reduction:
    @staticmethod
    def scratch(stages, columns, dtype):
        shapes = []
        for size, _, rows, scattered in stages:
            part = rows // size if scattered else rows
            shapes += [
                pltpu.VMEM((rows, columns), dtype),
                pltpu.VMEM((size, part, columns), dtype),
                pltpu.VMEM((rows, columns), dtype),
                pltpu.SemaphoreType.DMA((4, size)),
            ]
        return shapes

    def __init__(self, stages, refs):
        self.stages = stages
        self.levels = [refs[4 * i : 4 * i + 4] for i in range(len(stages))]

    def source(self):
        return self.levels[0][0]

    def total(self):
        return self.levels[0][2]

    def send(self, index):
        stage = self.stages[index]
        size, _, rows, scattered = stage
        source, received, _, sems = self.levels[index]
        place, others = peers_of(stage)
        part = rows // size if scattered else rows
        self.flying = []
        for step, (there, device) in enumerate(others):
            cut = source
            if scattered:
                cut = source.at[pl.ds(pl.multiple_of(there * part, part), part), :]
            copy = pltpu.make_async_remote_copy(
                src_ref=cut,
                dst_ref=received.at[place],
                send_sem=sems.at[0, step],
                recv_sem=sems.at[1, step],
                device_id={"dom": device},
                device_id_type=MESH,
            )
            copy.start()
            self.flying.append(copy)
        if scattered:
            received[place] = source[pl.ds(pl.multiple_of(place * part, part), part), :]
        else:
            received[place] = source[...]

    def fold(self, index):
        size, _, rows, scattered = self.stages[index]
        source, received, gathered, _ = self.levels[index]
        for copy in self.flying:
            copy.wait()
        total = received[0].astype(F32)
        for slot in range(1, size):
            total = total + received[slot].astype(F32)
        total = total.astype(source.dtype)
        if index + 1 < len(self.stages):
            self.levels[index + 1][0][...] = total
        else:
            self.place(index, total)

    def place(self, index, value):
        size, _, rows, scattered = self.stages[index]
        gathered = self.levels[index][2]
        if scattered:
            part = rows // size
            place, _ = peers_of(self.stages[index])
            gathered[pl.ds(pl.multiple_of(place * part, part), part), :] = value
        else:
            gathered[...] = value

    def gather(self, index):
        stage = self.stages[index]
        size, _, rows, scattered = stage
        gathered, sems = self.levels[index][2:]
        self.flying = []
        if not scattered:
            return
        part = rows // size
        place, others = peers_of(stage)
        mine = gathered.at[pl.ds(pl.multiple_of(place * part, part), part), :]
        for step, (_, device) in enumerate(others):
            copy = pltpu.make_async_remote_copy(
                src_ref=mine,
                dst_ref=mine,
                send_sem=sems.at[2, step],
                recv_sem=sems.at[3, step],
                device_id={"dom": device},
                device_id_type=MESH,
            )
            copy.start()
            self.flying.append(copy)

    def settle(self, index):
        for copy in self.flying:
            copy.wait()
        if index > 0:
            self.place(index - 1, self.levels[index][2][...])

    def last(self):
        return len(self.stages) - 1


def layer_kernel(
    token_stages,
    grad_stages,
    scale,
    counts_hbm,
    cells_hbm,
    cot_hbm,
    wx_hbm,
    wfx_hbm,
    wslice_hbm,
    wtemp_hbm,
    wqkv_hbm,
    wout_hbm,
    result_hbm,
    gcells_hbm,
    gwx_hbm,
    gwfx_hbm,
    gslice_hbm,
    gtemp_hbm,
    gqkv_hbm,
    gout_hbm,
    counts_ref,
    cells_ref,
    cot_ref,
    wx_ref,
    wfx_ref,
    wslice_ref,
    wtemp_ref,
    wqkv_ref,
    wout_ref,
    result_ref,
    gcells_ref,
    gwx_ref,
    gwfx_ref,
    gslice_ref,
    gtemp_ref,
    gqkv_ref,
    gout_ref,
    in_sems,
    out_sems,
    proj_ref,
    pair_ref,
    weight_ref,
    prob_ref,
    slope_ref,
    scaled_ref,
    inverse_ref,
    sigmoid_ref,
    cells_t,
    cot_t,
    proj_t,
    hidden_ref,
    dfeat_ref,
    dproj_ref,
    dlogit_ref,
    dtemp_ref,
    slice_bd,
    temp_bd,
    temp_row,
    same_head,
    maps_ref,
    acc_tokens,
    both_bd,
    both_t,
    slice_t,
    wout_t,
    wx_t,
    wfx_t,
    *sum_refs,
):
    rows = cells_ref.shape[0]
    chunks = rows // CHUNK
    middle = chunks // 2
    levels = 4 * len(token_stages)
    levels_g = 4 * len(grad_stages)
    token_sums = [
        Reduction(token_stages, sum_refs[i * levels : (i + 1) * levels]) for i in range(2)
    ]
    sum_refs = sum_refs[2 * levels :]
    early_sum, late_sum, last_sum = [
        Reduction(grad_stages, sum_refs[i * levels_g : (i + 1) * levels_g]) for i in range(3)
    ]

    pairs = (
        (wslice_hbm, wslice_ref),
        (wtemp_hbm, wtemp_ref),
        (cells_hbm, cells_ref),
        (wx_hbm, wx_ref),
        (counts_hbm, counts_ref),
        (wfx_hbm, wfx_ref),
        (wout_hbm, wout_ref),
        (cot_hbm, cot_ref),
        (wqkv_hbm, wqkv_ref),
    )
    incoming = [
        pltpu.make_async_copy(there, here, in_sems.at[i]) for i, (there, here) in enumerate(pairs)
    ]
    for copy in incoming:
        copy.start()
    barrier = pltpu.get_barrier_semaphore()
    greeted = 0
    for stage in token_stages:
        for _, device in peers_of(stage)[1]:
            pl.semaphore_signal(barrier, inc=1, device_id={"dom": device}, device_id_type=MESH)
            greeted += 1
    outgoing = []

    def put(source, target):
        copy = pltpu.make_async_copy(source, target, out_sems.at[len(outgoing)])
        copy.start()
        outgoing.append(copy)

    repeat32 = (
        (lax.broadcasted_iota(jnp.int32, (HEAD, HALF), 1) % HEAD)
        == lax.broadcasted_iota(jnp.int32, (HEAD, HALF), 0)
    ).astype(BF16)
    repeat64 = (
        (lax.broadcasted_iota(jnp.int32, (SLICES, 256), 1) % SLICES)
        == lax.broadcasted_iota(jnp.int32, (SLICES, 256), 0)
    ).astype(BF16)
    lane_head = lax.broadcasted_iota(jnp.int32, (256, 128), 1)
    row_head = lax.broadcasted_iota(jnp.int32, (256, 128), 0) // SLICES
    gather_heads = [(row_head + 4 * half == lane_head).astype(BF16) for half in range(2)]
    spread_lane = lax.broadcasted_iota(jnp.int32, (128, 256), 1) // SLICES
    spread_row = lax.broadcasted_iota(jnp.int32, (128, 256), 0)
    spread_heads = [(spread_lane + 4 * half == spread_row).astype(BF16) for half in range(2)]
    half_diag = block_mask((256, HALF), SLICES, HEAD)
    same_head[...] = block_mask((256, 256), SLICES, SLICES).astype(BF16)

    incoming[0].wait()
    incoming[1].wait()
    tall = mm_tn(repeat32, wslice_ref[...]).astype(BF16)
    slice_bd[...] = jnp.where(
        block_mask((HALF, 256), HEAD, SLICES), mm(tall, repeat64), 0.0
    ).astype(BF16)
    temp_rows = jnp.broadcast_to(wtemp_ref[...], (128, HEAD))
    column = mm_nt(repeat32.T, temp_rows)
    line = mm(temp_rows, repeat32)
    for half in range(2):
        place = slice(half * HALF, (half + 1) * HALF)
        lanes = lax.broadcasted_iota(jnp.int32, (HALF, 128), 1)
        heads = lax.broadcasted_iota(jnp.int32, (HALF, 128), 0) // HEAD + 4 * half
        temp_bd[place, :] = jnp.where(lanes == heads, column, 0.0).astype(BF16)
        heads = lax.broadcasted_iota(jnp.int32, (128, HALF), 1) // HEAD + 4 * half
        here = lax.broadcasted_iota(jnp.int32, (128, HALF), 0)
        temp_row[:, place] = jnp.where(here == heads, line, 0.0).astype(BF16)
    for copy in incoming[2:]:
        copy.wait()
    wout_t[...] = wout_ref[...].T
    count = counts_ref[0]

    def cut(index):
        return slice(index * CHUNK, (index + 1) * CHUNK)

    def project(index, carry):
        part = cut(index)
        cells = cells_ref[part, :]
        cells_t[:, part] = cells.T
        cot_t[:, part] = cot_ref[part, :].T
        projected = mm(cells, wx_ref[...]).astype(BF16)
        features = mm(cells, wfx_ref[...]).astype(BF16)
        d_hidden = mm(cot_ref[part, :], wout_t[...]).astype(BF16)
        temp_lin = mm(projected, temp_bd[...])
        away = jnp.exp(-jnp.abs(temp_lin))
        temper = 0.5 + (jnp.maximum(temp_lin, 0.0) + jnp.log(1.0 + away))
        proj_ref[part, :] = projected
        proj_t[:, part] = projected.T
        inverse_ref[part, :] = 1.0 / temper
        sigmoid_ref[part, :] = jnp.where(temp_lin >= 0.0, 1.0, away) / (1.0 + away)
        for half in range(2):
            lanes = slice(half * HALF, (half + 1) * HALF)
            pair_ref[part, half * 256 : half * 256 + HALF] = d_hidden[:, lanes]
            pair_ref[part, half * 256 + HALF : half * 256 + 256] = features[:, lanes]
        return carry

    def forward(half, index, carry):
        part = cut(index)
        lanes = slice(half * HALF, (half + 1) * HALF)
        span = slice(half * 256, (half + 1) * 256)
        place = lax.broadcasted_iota(jnp.int32, (CHUNK, 1), 0) + index * CHUNK
        live = (place < count).astype(F32)
        bent = jnp.tanh(mm(proj_ref[part, lanes], slice_bd[...]) * 0.1)
        cool = pick2(inverse_ref[part, :], spread_heads[half])
        scaled = (10.0 * bent) * cool
        powers = jnp.exp(scaled)
        sums = pick2(powers, same_head[...])
        over = pl.reciprocal(sums, approx=True)
        over = over * (2.0 - sums * over)
        probs = powers * (live * over)
        weights = probs.astype(BF16)
        weight_ref[part, span] = weights
        prob_ref[part, span] = probs
        slope_ref[part, span] = (1.0 - bent * bent) * cool
        scaled_ref[part, span] = scaled
        return carry

    lane = lax.broadcasted_iota(jnp.int32, (SLICES, 128), 1)

    def pay(half):
        payload = token_sums[half].source()
        span = slice(half * 256, (half + 1) * 256)
        right = jnp.concatenate([pair_ref[:, span], jnp.ones((rows, 128), BF16)], axis=1)
        acc_tokens[half] = mm_tn(weight_ref[:, span], right)
        dmix = jnp.where(half_diag, acc_tokens[half, :, 0:HALF], 0.0)
        numer = jnp.where(half_diag, acc_tokens[half, :, HALF : 2 * HALF], 0.0)
        payload[0:SLICES, 0:HALF] = sum(numer[i * 64 : i * 64 + 64] for i in range(4))
        payload[SLICES : 2 * SLICES, 0:HALF] = sum(dmix[i * 64 : i * 64 + 64] for i in range(4))
        totals = jnp.zeros((SLICES, 128), F32)
        for i in range(4):
            block = acc_tokens[half, i * 64 : i * 64 + 64, 2 * HALF : 2 * HALF + 128]
            totals = totals + jnp.where(lane == i, block, 0.0)
        payload[0:SLICES, HALF : HALF + 128] = totals
        payload[SLICES : 2 * SLICES, HALF : HALF + 128] = jnp.zeros((SLICES, 128), F32)

    diag_square = block_mask((HALF, HALF), HEAD, HEAD)

    def prepare_maps():
        for k in range(3):
            square = mm(mm_tn(repeat32, wqkv_ref[k]).astype(BF16), repeat32)
            maps_ref[k] = jnp.where(diag_square, square, 0.0).astype(BF16)
        slice_t[...] = slice_bd[...].T
        wx_t[...] = wx_ref[...].T
        wfx_t[...] = wfx_ref[...].T

    def steps(reduction):
        count_of_stages = len(reduction.stages)
        for index in range(count_of_stages):
            reduction.send(index)
            yield
            reduction.fold(index)
        for index in reversed(range(count_of_stages)):
            reduction.gather(index)
            yield
            reduction.settle(index)

    def finish(moves):
        for _ in moves:
            pass

    def expand(value):
        return jnp.where(half_diag, jnp.concatenate([value] * 4, axis=0), 0.0)

    def contract(value):
        value = jnp.where(half_diag, value, 0.0)
        return sum(value[i * SLICES : (i + 1) * SLICES] for i in range(4))

    def pick_back(value, weight):
        high, low = split(value)
        return mm_nt(high, weight) + mm_nt(low, weight)

    root = 1.0 / math.sqrt(HEAD)

    def attend(half):
        total = token_sums[half].total()
        numerators = total[0:SLICES, 0:HALF]
        d_mixed = total[SLICES : 2 * SLICES, 0:HALF]
        spread32 = block_mask((128, HALF), 1, HEAD).astype(BF16)
        denominators = pick3(total[0:SLICES, HALF : HALF + 128], spread32) + 1e-05
        tokens = numerators / denominators
        queries, key_rows, value_rows = [pick2(tokens, maps_ref[k]) for k in range(3)]
        keys_bd = expand(key_rows)
        values_bd = expand(value_rows)
        d_attention = wide(d_mixed, values_bd, mm_nt)
        bent = jnp.tanh(wide(queries, keys_bd, mm_nt) * (root / 10.0))
        powers = jnp.exp(10.0 * bent)
        attention = powers / pick2(powers, same_head[...])
        mixed_half = expand(wide(attention, values_bd, mm)).astype(BF16)
        shared = attention * d_attention
        shared = shared - attention * pick2(shared, same_head[...])
        d_scores = shared * (1.0 - bent * bent) * root
        d_queries = wide(d_scores, keys_bd, mm)
        d_keys = contract(wide(d_scores, queries, mm_tn))
        d_values = contract(wide(attention, d_mixed, mm_tn))
        d_maps = (d_queries, d_keys, d_values)
        d_tokens = sum(pick_back(d_maps[k], maps_ref[k]) for k in range(3))
        d_numer = d_tokens / denominators
        dnumer_half = expand(d_numer).astype(BF16)
        both = jnp.concatenate([mixed_half, dnumer_half], axis=1)
        both_bd[half] = both
        both_t[half] = both.T
        high, low = split(expand(d_numer * tokens))
        ones = jnp.ones((128, HALF), BF16)
        d_denom = -(mm_nt(ones, high) + mm_nt(ones, low))[0:1, :]
        return tokens, d_maps, d_denom

    def early(half, index, carry):
        part = cut(index)
        lanes = slice(half * HALF, (half + 1) * HALF)
        made = mm(weight_ref[part, half * 256 : (half + 1) * 256], both_bd[half]).astype(BF16)
        hidden_ref[part, lanes] = made[:, 0:HALF]
        dfeat_ref[part, lanes] = made[:, HALF : 2 * HALF]
        return carry

    def fill_early(half, target):
        lanes = slice(half * HALF, (half + 1) * HALF)
        target[:, 0:128] = mm(cot_t[...], hidden_ref[:, lanes]).astype(BF16)
        target[:, 128:256] = mm(cells_t[...], dfeat_ref[:, lanes]).astype(BF16)

    def backward(half, d_denom, index, carry):
        part = cut(index)
        lanes = slice(half * HALF, (half + 1) * HALF)
        span = slice(half * 256, (half + 1) * 256)
        d_weights = mm(pair_ref[part, span], both_t[half]) + d_denom
        probs = prob_ref[part, span]
        shared = probs * d_weights
        shared = shared - probs * pick2(shared, same_head[...])
        d_logits = (shared * slope_ref[part, span]).astype(BF16)
        d_temper = -pick2(shared * scaled_ref[part, span], gather_heads[half])
        d_temp = (d_temper * inverse_ref[part, :] * sigmoid_ref[part, :]).astype(BF16)
        dlogit_ref[part, :] = d_logits
        dtemp_ref[part, :] = d_temp
        dproj_ref[part, lanes] = (
            mm(d_logits, slice_t[...]) + mm(d_temp, temp_row[:, lanes])
        ).astype(BF16)
        return carry

    def fill_late(half, target, start):
        lanes = slice(half * HALF, (half + 1) * HALF)
        block = mm(proj_t[lanes, :], dlogit_ref[...])
        block = jnp.where(block_mask((HALF, 256), HEAD, SLICES), block, 0.0)
        block = block[:, 0:128] + block[:, 128:256]
        block = block + pltpu.roll(block, 64, 1)
        here = lax.broadcasted_iota(jnp.int32, (HALF, 128), 1)
        heads = lax.broadcasted_iota(jnp.int32, (HALF, 128), 0) // HEAD + 4 * half
        own = jnp.where(here == heads, mm(proj_t[lanes, :], dtemp_ref[...]), 0.0)
        own = jnp.sum(own, axis=1, keepdims=True)
        extra = slice(start + 128, start + 256)
        target[:, start : start + 128] = mm(cells_t[...], dproj_ref[:, lanes]).astype(BF16)
        target[0:HALF, extra] = jnp.where(here < SLICES, block, own).astype(BF16)
        target[HALF:WIDTH, extra] = jnp.zeros((WIDTH - HALF, 128), BF16)

    def results(index, carry):
        part = cut(index)
        result_ref[part, :] = mm(hidden_ref[part, :], wout_ref[...]).astype(BF16)
        return carry

    def cell_grads(index, carry):
        part = cut(index)
        gcells_ref[part, :] = (
            mm(dproj_ref[part, :], wx_t[...]) + mm(dfeat_ref[part, :], wfx_t[...])
        ).astype(BF16)
        return carry

    def loop(step, first=0, end=chunks):
        for index in range(first, end):
            step(index, 0)

    bind = functools.partial
    loop(project)
    loop(bind(forward, 0))
    pay(0)
    pl.semaphore_wait(barrier, greeted)
    first_moves, second_moves = [steps(reduction) for reduction in token_sums]
    next(first_moves)
    loop(bind(forward, 1), 0, middle)
    next(first_moves)
    loop(bind(forward, 1), middle, chunks)
    pay(1)
    next(second_moves)
    next(first_moves)
    prepare_maps()
    next(second_moves)
    next(first_moves)
    finish(first_moves)

    tokens0, d_maps0, d_denom0 = attend(0)
    next(second_moves)
    loop(bind(early, 0))
    loop(bind(backward, 0, d_denom0), 0, middle)
    next(second_moves)
    loop(bind(backward, 0, d_denom0), middle, chunks)
    fill_early(0, early_sum.source())
    fill_late(0, early_sum.source(), 256)
    early_moves, late_moves, last_moves = [
        steps(reduction) for reduction in (early_sum, late_sum, last_sum)
    ]
    next(early_moves)
    finish(second_moves)

    tokens1, d_maps1, d_denom1 = attend(1)
    next(early_moves)
    loop(bind(early, 1))
    fill_early(1, late_sum.source())
    next(late_moves)
    loop(bind(backward, 1, d_denom1), 0, middle)
    next(early_moves)
    next(late_moves)
    loop(bind(backward, 1, d_denom1), middle, chunks)
    fill_late(1, last_sum.source(), 0)
    next(last_moves)
    next(early_moves)
    next(late_moves)
    loop(cell_grads)
    put(gcells_ref, gcells_hbm)
    next(last_moves)
    finish(early_moves)
    next(late_moves)
    loop(results)
    put(result_ref, result_hbm)
    for k in range(3):
        square = wide(tokens0, d_maps0[k], mm_tn) + wide(tokens1, d_maps1[k], mm_tn)
        square = jnp.where(diag_square, square, 0.0)
        strip = sum(square[i * HEAD : (i + 1) * HEAD] for i in range(4))
        gqkv_ref[k] = pick2(strip, repeat32.T) * scale
    put(gqkv_ref, gqkv_hbm)
    gwfx_ref[:, 0:HALF] = early_sum.total()[:, 128:256].astype(F32) * scale
    gout_ref[0:HALF, :] = early_sum.total()[:, 0:128].astype(F32).T * scale
    gwx_ref[:, 0:HALF] = early_sum.total()[:, 256:384].astype(F32) * scale
    next(last_moves)
    finish(late_moves)
    gwfx_ref[:, HALF:WIDTH] = late_sum.total()[:, 128:256].astype(F32) * scale
    put(gwfx_ref, gwfx_hbm)
    gout_ref[HALF:WIDTH, :] = late_sum.total()[:, 0:128].astype(F32).T * scale
    put(gout_ref, gout_hbm)
    next(last_moves)
    finish(last_moves)
    gwx_ref[:, HALF:WIDTH] = last_sum.total()[:, 0:HALF].astype(F32) * scale
    put(gwx_ref, gwx_hbm)
    extra = early_sum.total()[0:HALF, 384:512].astype(F32)
    extra = extra + last_sum.total()[0:HALF, 128:256].astype(F32)
    extra = sum(extra[i * HEAD : (i + 1) * HEAD] for i in range(4)) * scale
    gslice_ref[...] = extra[:, 0:SLICES]
    put(gslice_ref, gslice_hbm)
    unit = (
        lax.broadcasted_iota(jnp.int32, (HEAD, HEAD), 0)
        == lax.broadcasted_iota(jnp.int32, (HEAD, HEAD), 1)
    ).astype(BF16)
    gtemp_ref[...] = pick3(extra, unit, mm_tn)[SLICES : SLICES + 1, :]
    put(gtemp_ref, gtemp_hbm)
    for copy in outgoing:
        copy.wait()


def hand_over(*refs):
    count = (len(refs) - 2) // 3
    sources, targets, between = refs[:count], refs[count : 2 * count], refs[2 * count : 3 * count]
    arrive, leave = refs[-2:]
    copies = [pltpu.make_async_copy(sources[i], between[i], arrive.at[i]) for i in range(count)]
    for copy in copies:
        copy.start()
    onward = []
    for i, copy in enumerate(copies):
        copy.wait()
        onward.append(pltpu.make_async_copy(between[i], targets[i], leave.at[i]))
        onward[-1].start()
    for copy in onward:
        copy.wait()


def body(devices, cells, counts, w_x, w_fx, w_slice, w_temp, w_qkv, w_out, cotangent):
    rows = cells.shape[0]
    token_stages = stages_of(devices, 2 * SLICES, 8)
    grad_stages = stages_of(devices, WIDTH, 16)
    scale = 1.0 / math.sqrt(rows * devices)
    anywhere = pl.BlockSpec(memory_space=pl.ANY)
    vmem = pltpu.VMEM
    out_shapes = [
        ((rows, WIDTH), BF16),
        ((rows, WIDTH), BF16),
        ((WIDTH, WIDTH), F32),
        ((WIDTH, WIDTH), F32),
        ((HEAD, SLICES), F32),
        ((1, HEAD), F32),
        ((3, HEAD, HEAD), F32),
        ((WIDTH, WIDTH), F32),
    ]
    out_shape = tuple(jax.ShapeDtypeStruct(*one) for one in out_shapes)
    outs = pl.pallas_call(
        functools.partial(layer_kernel, token_stages, grad_stages, scale),
        out_shape=out_shape,
        in_specs=[anywhere] * 9,
        out_specs=[anywhere] * 8,
        scratch_shapes=[
            pltpu.SMEM((1,), jnp.int32),
            vmem((rows, WIDTH), BF16),
            vmem((rows, WIDTH), BF16),
            vmem((WIDTH, WIDTH), BF16),
            vmem((WIDTH, WIDTH), BF16),
            vmem((HEAD, SLICES), BF16),
            vmem((1, HEAD), BF16),
            vmem((3, HEAD, HEAD), BF16),
            vmem((WIDTH, WIDTH), BF16),
        ]
        + [vmem(*one) for one in out_shapes]
        + [
            pltpu.SemaphoreType.DMA((9,)),
            pltpu.SemaphoreType.DMA((8,)),
            vmem((rows, WIDTH), BF16),
            vmem((rows, SPREAD), BF16),
            vmem((rows, SPREAD), BF16),
            vmem((rows, SPREAD), F32),
            vmem((rows, SPREAD), F32),
            vmem((rows, SPREAD), F32),
            vmem((rows, 128), F32),
            vmem((rows, 128), F32),
            vmem((WIDTH, rows), BF16),
            vmem((WIDTH, rows), BF16),
            vmem((WIDTH, rows), BF16),
            vmem((rows, WIDTH), BF16),
            vmem((rows, WIDTH), BF16),
            vmem((rows, WIDTH), BF16),
            vmem((rows, 256), BF16),
            vmem((rows, 128), BF16),
            vmem((HALF, 256), BF16),
            vmem((WIDTH, 128), BF16),
            vmem((128, WIDTH), BF16),
            vmem((256, 256), BF16),
            vmem((3, HALF, HALF), BF16),
            vmem((2, 256, 2 * HALF + 128), F32),
            vmem((2, 256, 2 * HALF), BF16),
            vmem((2, 256, 2 * HALF), BF16),
            vmem((256, HALF), BF16),
            vmem((WIDTH, WIDTH), BF16),
            vmem((WIDTH, WIDTH), BF16),
            vmem((WIDTH, WIDTH), BF16),
        ]
        + Reduction.scratch(token_stages, HALF + 128, F32) * 2
        + Reduction.scratch(grad_stages, 2 * WIDTH, BF16)
        + Reduction.scratch(grad_stages, 256, BF16)
        + Reduction.scratch(grad_stages, 256, BF16),
        compiler_params=pltpu.CompilerParams(
            collective_id=0, has_side_effects=True, vmem_limit_bytes=60 * 1024 * 1024
        ),
    )(counts, cells, cotangent, w_x, w_fx, w_slice, w_temp.reshape(1, HEAD), w_qkv, w_out)
    outs = pl.pallas_call(
        hand_over,
        out_shape=out_shape,
        in_specs=[anywhere] * 8,
        out_specs=[anywhere] * 8,
        scratch_shapes=[vmem(*one) for one in out_shapes] + [pltpu.SemaphoreType.DMA((8,))] * 2,
        compiler_params=pltpu.CompilerParams(vmem_limit_bytes=60 * 1024 * 1024),
    )(*outs)
    result, gcells, gwx, gwfx, gslice, gtemp, gqkv, gout = outs
    return result, gcells, gwx, gwfx, gslice, gtemp.reshape(HEAD), gqkv, gout


def solution(mesh):
    placed = (
        P(("groups", "dom"), None),
        P(("groups", "dom")),
        P(),
        P(),
        P(),
        P(),
        P(),
        P(),
        P(("groups", "dom"), None),
    )
    return jax.shard_map(
        functools.partial(body, mesh.shape["dom"]),
        mesh=mesh,
        in_specs=placed,
        out_specs=(
            P(("groups", "dom"), None),
            P(("groups", "dom"), None),
            P("groups", None),
            P("groups", None),
            P("groups", None),
            P("groups"),
            P("groups", None, None),
            P("groups", None),
        ),
        check_vma=False,
    )
```
